32 devices in a mesh: replica: 8 (over y, x, core), group: 4 (over z).
Axes of the slice: x: 2, y: 2, z: 4, core: 2. Of those that a mesh axis runs over, the one named last changes fastest.
Arguments:
- tokens: bfloat16 [8192, 768], P(('replica', 'group')), may hold values from -6 to 6
- segment: int32 [8192], P(('replica', 'group')), may hold values from 0 to 255, as said below
- g_attn: bfloat16 [768], P('group'), may hold values from 0.5 to 1.5
- w_qkv: bfloat16 [768, 2304], P('group'), may hold values from -0.21875 to 0.21875
- w_out: bfloat16 [768, 768], P('group'), may hold values from -0.625 to 0.625
- g_mlp: bfloat16 [768], P('group'), may hold values from 0.5 to 1.5
- w_in: bfloat16 [768, 2304], P('group'), may hold values from -0.21875 to 0.21875
- w_down: bfloat16 [1152, 768], P('group'), may hold values from -0.1875 to 0.1875
- grad_out: bfloat16 [8192, 768], P(('replica', 'group')), may hold values from -6 to 6
Outputs:
- output: bfloat16 [8192, 768], P(('replica', 'group'))
- tokens_grad: bfloat16 [8192, 768], P(('replica', 'group'))
- g_attn_grad: float32 [768], P('group')
- w_qkv_grad: float32 [768, 2304], P('group')
- w_out_grad: float32 [768, 768], P('group')
- g_mlp_grad: float32 [768], P('group')
- w_in_grad: float32 [768, 2304], P('group')
- w_down_grad: float32 [1152, 768], P('group')
The draws below stay inside these ranges and needn't reach their ends.
Inputs may be any that keep to these rules, and one draw needn't show every extreme that they name: Within each block of 256 rows segment starts at 0 and rises by 0 or 1 from row to row; in every draw some block is one sequence of 256 tokens and some other block is 256 sequences of one token.
All inputs are finite; a program needn't handle non-finite values.
Results may differ from the reference program's by a relative error of at most 0.015.
Values may be sent and summed in bfloat16 or wider, within the bound.
No kernel may reach another device: no remote copies, remote signals or barrier semaphores. Data moves between devices by JAX's collectives and lax.ppermute only.
A program may use at most 128 MiB of HBM per device.

```python
import jax
import jax.numpy as jnp
from jax import lax

D = 768
HEADS = 12
HEAD_DIM = 64
FF = 1152
TOK_DEV = 256
TOKENS = 8192


def draw_segment(key, part):
    key = jax.random.fold_in(key, 7)
    blocks = TOKENS // TOK_DEV
    level_key, flag_key, pick_key, other_key = jax.random.split(key, 4)
    level = jax.random.randint(level_key, (blocks, 1), 0, 4)
    spacing = jnp.maximum(TOK_DEV // 4 ** level, 1)
    raw_bits = jax.random.randint(flag_key, (blocks, TOK_DEV), 0, 1 << 30)
    starts = raw_bits % spacing == 0
    whole_block = jax.random.randint(pick_key, (), 0, blocks)
    offset = jax.random.randint(other_key, (), 1, blocks)
    single_block = (whole_block + offset) % blocks
    block_ids = jnp.arange(blocks)[:, None]
    column_ids = jnp.arange(TOK_DEV)[None, :]
    starts = jnp.where(block_ids == whole_block, False, starts)
    starts = jnp.where(block_ids == single_block, True, starts)
    starts = jnp.where(column_ids == 0, True, starts)
    numbers = jnp.cumsum(starts.astype(jnp.int32), axis=1) - 1
    return numbers.reshape(TOKENS).astype(jnp.int32)


def shard_levels(stream_key, shape, cuts, least, top_value):
    def one(dim, shards_of):
        steps = jax.random.uniform(jax.random.fold_in(jax.random.fold_in(stream_key, 6), dim), (shards_of,), jnp.float32, least / len(cuts), top_value / len(cuts))
        return jnp.repeat(jnp.exp(steps), shape[dim] // shards_of).reshape((-1,) + (1,) * (len(shape) - dim - 1))

    factor_of = one(*cuts[0])
    for cut in cuts[1:]:
        factor_of = factor_of * one(*cut)
    return factor_of


def normal_values(key, extent, deviation, most, cuts=(), kind=jnp.bfloat16):
    drawn = jax.random.normal(key, extent, jnp.float32) * deviation
    if len(cuts) > 0:
        drawn = shard_levels(key, extent, cuts, -0.22, 0.18) * drawn
    return jnp.clip(drawn, min=-most, max=most).astype(kind)


def setup_inputs(seed: int = 0) -> dict:
    key_list = jax.random.split(jax.random.key(seed), 10)
    tokens = normal_values(key_list[0], (TOKENS, D), 1.0, 6.0, ((0, 32),))
    segment = draw_segment(jax.random.fold_in(key_list[9], 71), 0)
    g_attn = jnp.clip(1.0 + 0.1 * jax.random.normal(key_list[2], (D,), jnp.float32), 0.5, 1.5).astype(jnp.bfloat16)
    w_qkv = normal_values(key_list[3], (D, 3 * D), D ** -0.5, 0.21875, ((0, 4),))
    w_out = normal_values(key_list[4], (D, D), (D // 8) ** -0.5, 0.625, ((0, 4),))
    g_mlp = jnp.clip(1.0 + 0.1 * jax.random.normal(key_list[5], (D,), jnp.float32), 0.5, 1.5).astype(jnp.bfloat16)
    w_in = normal_values(key_list[6], (D, 2 * FF), D ** -0.5, 0.21875, ((0, 4),))
    w_down = normal_values(key_list[7], (FF, D), FF ** -0.5, 0.1875, ((0, 4),))
    grad_out = normal_values(key_list[8], (TOKENS, D), 1.0, 6.0, ((0, 32),))
    return {"tokens": tokens, "segment": segment, "g_attn": g_attn, "w_qkv": w_qkv, "w_out": w_out, "g_mlp": g_mlp, "w_in": w_in, "w_down": w_down, "grad_out": grad_out}


@jax.custom_vjp
def low(v):
    return lax.optimization_barrier(v.astype(jnp.bfloat16)).astype(jnp.float32)

@jax.custom_vjp
def low_back(v):
    return v

def low_keep(v):
    return (low(v), None)

def low_pass(kept, grad):
    return (grad,)

def back_keep(v):
    return (v, None)

def back_low(kept, grad):
    return (low(grad),)
low.defvjp(low_keep, low_pass)
low_back.defvjp(back_keep, back_low)
norm_eps = 1e-05
rope_base = 160000.0
highest = lax.Precision.HIGHEST

def token_positions(segment):
    length = segment.shape[0]
    index = jnp.arange(length, dtype=jnp.int32)
    before = jnp.concatenate([jnp.full((1,), -1, jnp.int32), segment[:-1]])
    first = lax.cummax(jnp.where(segment != before, index, 0), axis=0)
    return index - first

def rotary_tables(position):
    half_dim = HEAD_DIM // 2
    inverse = rope_base ** (-(jnp.arange(half_dim, dtype=jnp.float32) * 2.0 / HEAD_DIM))
    angles = position.astype(jnp.float32)[:, None] * inverse[None, :]
    angles = jnp.concatenate([angles, angles], axis=1)
    return (jnp.cos(angles)[:, None, :], jnp.sin(angles)[:, None, :])

def rotate_half(values):
    half_dim = values.shape[-1] // 2
    return jnp.concatenate([-values[..., half_dim:], values[..., :half_dim]], axis=-1)

def layer_norm(values, gain):
    centred = values - lax.optimization_barrier(jnp.mean(values, axis=1, keepdims=True))
    inverse = lax.rsqrt(lax.optimization_barrier(jnp.mean(centred * centred, axis=1, keepdims=True)) + norm_eps)
    return centred * inverse * gain

def layer_block(block_rows, block_segment, g_attn, w_qkv, w_out, g_mlp, w_in, w_down):
    length = block_rows.shape[0]
    position = token_positions(block_segment)
    cosine, sine = rotary_tables(position)
    attn_in = low(layer_norm(block_rows, g_attn))
    qkv = low_back(jnp.dot(attn_in, w_qkv, precision=highest))
    queries = qkv[:, :D].reshape(length, HEADS, HEAD_DIM)
    keys = qkv[:, D:2 * D].reshape(length, HEADS, HEAD_DIM)
    values = low(qkv[:, 2 * D:].reshape(length, HEADS, HEAD_DIM))
    queries = low(queries * cosine + rotate_half(queries) * sine)
    keys = low(keys * cosine + rotate_half(keys) * sine)
    scores = jnp.einsum('qhd,khd->hqk', queries, keys, precision=highest) * HEAD_DIM ** (-0.5)
    same_seq = (block_segment[:, None] == block_segment[None, :])[None]
    scores = low_back(jnp.where(same_seq, scores, -1e+30))
    row_top = lax.optimization_barrier(jnp.max(scores, axis=2, keepdims=True))
    weights_exp = jnp.exp(scores - row_top)
    probs = low(weights_exp / lax.optimization_barrier(jnp.sum(weights_exp, axis=2, keepdims=True)))
    mixed = jnp.einsum('hqk,khd->qhd', probs, values, precision=highest).reshape(length, D)
    mixed = low(low_back(mixed))
    middle = block_rows + low_back(jnp.dot(mixed, w_out, precision=highest))
    mlp_in = low(layer_norm(middle, g_mlp))
    gate_up = low_back(jnp.dot(mlp_in, w_in, precision=highest))
    hidden = low(jax.nn.gelu(gate_up[:, :FF], approximate=False) * gate_up[:, FF:])
    return middle + low_back(jnp.dot(hidden, w_down, precision=highest))

def reference(tokens, segment, g_attn, w_qkv, w_out, g_mlp, w_in, w_down, grad_out):
    blocks = tokens.shape[0] // TOK_DEV
    params = tuple((p.astype(jnp.float32) for p in (g_attn, w_qkv, w_out, g_mlp, w_in, w_down)))
    stepper = jax.checkpoint(layer_block)
    block_segments = segment.reshape(blocks, TOK_DEV)

    def forward(rows, weights):

        def scan_step(carry, item):
            return (carry, stepper(item[0], item[1], *weights))
        _, outputs = lax.scan(scan_step, None, (rows.reshape(blocks, TOK_DEV, D), block_segments))
        return outputs.reshape(blocks * TOK_DEV, D)
    result, pull = jax.vjp(forward, tokens.astype(jnp.float32), params)
    rows_grad, weight_grads = pull(grad_out.astype(jnp.float32))
    return (result.astype(jnp.bfloat16), rows_grad.astype(jnp.bfloat16), weight_grads[0], weight_grads[1], weight_grads[2], weight_grads[3], weight_grads[4], weight_grads[5])
```

```python
import functools

import jax
import jax.numpy as jnp
from jax import lax
from jax.experimental import pallas as pl
from jax.experimental.pallas import tpu as pltpu
from jax.sharding import PartitionSpec as P

HEADS = 12
HEAD_DIM = 64
FF = 1152
D = 768
TILE = 384
PAIR = 128

norm_eps = 1e-05
rope_base = 160000.0
head_scale = HEAD_DIM ** (-0.5)
f32 = jnp.float32
bf16 = jnp.bfloat16

VMEM = pl.BlockSpec(memory_space=pltpu.VMEM)
SMEM = pl.BlockSpec(memory_space=pltpu.SMEM)


def run(body, name, outs, place, ins, scratch=(), flops=0):
    moved = sum(a.size * a.dtype.itemsize for a in ins)
    moved += sum(o.size * o.dtype.itemsize for o in outs)
    return pl.pallas_call(
        body,
        out_shape=outs,
        in_specs=[SMEM] + [VMEM] * len(ins),
        out_specs=[VMEM] * len(outs),
        scratch_shapes=list(scratch),
        compiler_params=pltpu.CompilerParams(vmem_limit_bytes=44 * 1024 * 1024),
        cost_estimate=pl.CostEstimate(flops=flops, bytes_accessed=moved, transcendentals=0),
        name=name,
    )(place, *ins)


def shape(dims, dtype=bf16):
    return jax.ShapeDtypeStruct(dims, dtype)


def dot(a, b):
    return lax.dot_general(a, b, (((1,), (0,)), ((), ())), preferred_element_type=f32)


def dot_bt(a, b):
    return lax.dot_general(a, b, (((1,), (1,)), ((), ())), preferred_element_type=f32)


def dot_at(a, b):
    return lax.dot_general(a, b, (((0,), (0,)), ((), ())), preferred_element_type=f32)


def token_positions(segment):
    length = segment.shape[0]
    index = jnp.arange(length, dtype=jnp.int32)
    before = jnp.concatenate([jnp.full((1,), -1, jnp.int32), segment[:-1]])
    first = lax.cummax(jnp.where(segment != before, index, 0), axis=0)
    return index - first


def rotary_tables(position):
    half_dim = HEAD_DIM // 2
    inverse = rope_base ** (-(jnp.arange(half_dim, dtype=f32) * 2.0 / HEAD_DIM))
    angles = position.astype(f32)[:, None] * inverse[None, :]
    cosine, sine = jnp.cos(angles), jnp.sin(angles)
    return (
        jnp.concatenate([cosine] * 4, axis=1),
        jnp.concatenate([-sine, sine, -sine, sine], axis=1),
    )


def rows(start, size, step=16):
    return pl.ds(pl.multiple_of(start, step), size)


def columns(start, size):
    return pl.ds(pl.multiple_of(start, 128), size)


def assemble(place, parts, full, own, groups, high, low, width, start):
    z, hb, lb, core = place[0], place[1], place[2], place[3]
    shard = own.shape[0]
    full[rows(z * shard, shard), :] = own[...]
    for index, part in enumerate(parts):
        flip_low, flip_high, other = index & 1, (index >> 1) & 1, index >> 2
        hi = (lb if other else hb) ^ flip_high
        lo = (hb if other else lb) ^ flip_low
        half = core ^ other
        for k in range(1, groups):
            group = lax.rem(z + groups - k, groups)
            at = group * shard + hi * high + lo * low
            full[rows(at, part.shape[1]), columns(half * width, width)] = part[
                k - 1, :, start : start + width
            ]


def norm_parts(values):
    centred = values - jnp.mean(values, axis=1, keepdims=True)
    inverse = lax.rsqrt(jnp.mean(centred * centred, axis=1, keepdims=True) + norm_eps)
    return centred * inverse, inverse


def norm_back(upstream, normed, inverse, gain):
    gain_grad = jnp.sum(upstream * normed, axis=0, keepdims=True)
    scaled = upstream * gain
    inner = (
        scaled
        - jnp.mean(scaled, axis=1, keepdims=True)
        - normed * jnp.mean(scaled * normed, axis=1, keepdims=True)
    )
    return inverse * inner, gain_grad


def swap_halves(u):
    lane = lax.broadcasted_iota(jnp.int32, u.shape, 1)
    return jnp.where(lane % HEAD_DIM < HEAD_DIM // 2, pltpu.roll(u, PAIR - 32, 1), pltpu.roll(u, 32, 1))


def head_masks():
    lane = lax.broadcasted_iota(jnp.int32, (1, PAIR), 1)
    first = (lane < HEAD_DIM).astype(f32)
    return first.astype(bf16), (1.0 - first).astype(bf16)


def attn_forward(groups, place, tok, gains, cosine, sine, seg_col, seg_row, own, *rest):
    parts, (attn_in, qkv, mixed, lse, w_full) = rest[:8], rest[8:]
    assemble(place, parts, w_full, own, groups, 96, 48, 3 * D // 2, 0)
    normed, _ = norm_parts(tok[...].astype(f32))
    attn_in[...] = (normed * gains[0:1, :]).astype(bf16)

    def turned(j, _):
        at = columns(j * TILE, TILE)
        raw = dot(attn_in[...], w_full[:, at])
        turned_parts = []
        for i in range(TILE // PAIR):
            u = raw[:, i * PAIR : (i + 1) * PAIR]
            turned_parts.append(u * cosine[...] + swap_halves(u) * sine[...])
        qkv[:, at] = jnp.concatenate(turned_parts, axis=1).astype(bf16)
        return 0

    lax.fori_loop(0, 4, turned, 0)

    def plain(j, _):
        at = columns(j * TILE, TILE)
        qkv[:, at] = dot(attn_in[...], w_full[:, at]).astype(bf16)
        return 0

    lax.fori_loop(4, 6, plain, 0)
    masks = head_masks()
    same = seg_col[...] == seg_row[...]
    lane = lax.broadcasted_iota(jnp.int32, (tok.shape[0], PAIR), 1)

    def pair(j, kept):
        q = qkv[:, columns(j * PAIR, PAIR)]
        k = qkv[:, columns(D + j * PAIR, PAIR)]
        v = qkv[:, columns(2 * D + j * PAIR, PAIR)]
        made = []
        for a in range(2):
            scores = dot_bt(q * masks[a], k) * head_scale
            scores = jnp.where(same, scores, -1e30)
            top = jnp.max(scores, axis=1, keepdims=True)
            e = jnp.exp(scores - top)
            total = jnp.sum(e, axis=1, keepdims=True)
            probs = (e * (1.0 / total)).astype(bf16)
            made.append(dot(probs, v))
            kept = jnp.where(lane == 2 * j + a, top + jnp.log(total), kept)
        mixed[:, columns(j * PAIR, PAIR)] = jnp.where(lane < HEAD_DIM, made[0], made[1]).astype(bf16)
        return kept

    lse[...] = lax.fori_loop(0, HEADS // 2, pair, jnp.zeros((tok.shape[0], PAIR), f32))


def mlp_forward(groups, place, tok, mixed, gains, own_in, own_out, *rest):
    parts, rest = rest[:8], rest[8:]
    middle, mlp_in, hidden, act, slope, w_in, w_out = rest
    assemble(place, parts, w_out, own_out, groups, 96, 48, D // 2, FF)
    assemble(place, parts, w_in, own_in, groups, 96, 48, FF, 0)
    for j in range(2):
        at = slice(j * TILE, (j + 1) * TILE)
        middle[:, at] = tok[:, at].astype(f32) + dot(mixed[...], w_out[:, at])
    normed, _ = norm_parts(middle[...])
    mlp_in[...] = (normed * gains[1:2, :]).astype(bf16)

    def step(j, _):
        at = columns(j * TILE, TILE)
        u = dot(mlp_in[...], w_in[:, at])
        gate = dot(mlp_in[...], w_in[:, columns(FF + j * TILE, TILE)])
        cdf = 0.5 + 0.5 * lax.erf(u * 0.7071067811865476)
        a = u * cdf
        act[:, at] = a
        slope[:, at] = gate * (cdf + u * (0.3989422804014327 * jnp.exp(-0.5 * u * u)))
        hidden[:, at] = (a * gate).astype(bf16)
        return 0

    lax.fori_loop(0, FF // TILE, step, 0)


def down_backward(groups, place, grad_out, hidden, middle, act, slope, own, *rest):
    parts, (output, gate_up_grad, w_down) = rest[:8], rest[8:]
    assemble(place, parts, w_down, own, groups, 144, 64, D // 2, 0)

    def step(j, _):
        at = columns(j * TILE, TILE)
        hidden_grad = dot_bt(grad_out[...], w_down[rows(j * TILE, TILE), :])
        gate_up_grad[:, at] = (hidden_grad * slope[:, at]).astype(bf16)
        gate_up_grad[:, columns(FF + j * TILE, TILE)] = (hidden_grad * act[:, at]).astype(bf16)
        return 0

    lax.fori_loop(0, FF // TILE, step, 0)
    for j in range(2):
        at = slice(j * TILE, (j + 1) * TILE)
        output[:, at] = (middle[:, at] + dot(hidden[...], w_down[:, at])).astype(bf16)


def mlp_backward(groups, place, gate_up_grad, grad_out, middle, gains, own_in, own_out, *rest):
    parts, rest = rest[:8], rest[8:]
    middle_grad, branch_grad, mixed_grad, gain_grad, w_in, w_out, total = rest
    assemble(place, parts, w_in, own_in, groups, 96, 48, FF, 0)
    assemble(place, parts, w_out, own_out, groups, 96, 48, D // 2, FF)

    def step(j, _):
        total[:, columns(j * 256, 256)] = dot_bt(gate_up_grad[...], w_in[rows(j * 256, 256), :])
        return 0

    lax.fori_loop(0, D // 256, step, 0)
    normed, inverse = norm_parts(middle[...])
    part, gain_grad[...] = norm_back(total[...], normed, inverse, gains[1:2, :])
    whole = grad_out[...].astype(f32) + part
    middle_grad[...] = whole
    branch_grad[...] = whole.astype(bf16)

    def back(j, _):
        mixed_grad[:, columns(j * 256, 256)] = dot_bt(
            branch_grad[...], w_out[rows(j * 256, 256), :]
        ).astype(bf16)
        return 0

    lax.fori_loop(0, D // 256, back, 0)


def attn_backward(place, qkv, lse, mixed_grad, cosine, sine, seg_col, seg_row, qkv_grad):
    masks = head_masks()
    same = seg_col[...] == seg_row[...]
    length = qkv.shape[0]
    lane = lax.broadcasted_iota(jnp.int32, (length, PAIR), 1)

    def pair(j, _):
        q = qkv[:, columns(j * PAIR, PAIR)]
        k = qkv[:, columns(D + j * PAIR, PAIR)]
        v = qkv[:, columns(2 * D + j * PAIR, PAIR)]
        upstream = mixed_grad[:, columns(j * PAIR, PAIR)]
        made = []
        for a in range(2):
            scores = dot_bt(q * masks[a], k) * head_scale
            log_total = jnp.sum(jnp.where(lane == 2 * j + a, lse[...], 0.0), axis=1, keepdims=True)
            probs = jnp.where(same, jnp.exp(scores - log_total), 0.0)
            prob_grad = dot_bt(upstream * masks[a], v)
            delta = jnp.sum(probs * prob_grad, axis=1, keepdims=True)
            score_grad = (probs * (prob_grad - delta)).astype(bf16)
            made.append(
                (
                    dot(score_grad, k),
                    dot_at(score_grad, q),
                    dot_at(probs.astype(bf16), upstream),
                )
            )
        first = lane < HEAD_DIM
        for i in range(2):
            u = jnp.where(first, made[0][i], made[1][i]) * head_scale
            u = u * cosine[...] - swap_halves(u) * sine[...]
            qkv_grad[:, columns(i * D + j * PAIR, PAIR)] = u.astype(bf16)
        qkv_grad[:, columns(2 * D + j * PAIR, PAIR)] = jnp.where(first, made[0][2], made[1][2]).astype(bf16)
        return 0

    lax.fori_loop(0, HEADS // 2, pair, 0)


def attn_in_backward(groups, place, qkv_grad, tok, middle_grad, gains, own, *rest):
    parts, (tokens_grad, gain_grad, w_full, total) = rest[:8], rest[8:]
    assemble(place, parts, w_full, own, groups, 96, 48, 3 * D // 2, 0)

    def step(j, _):
        total[:, columns(j * 256, 256)] = dot_bt(qkv_grad[...], w_full[rows(j * 256, 256), :])
        return 0

    lax.fori_loop(0, D // 256, step, 0)
    normed, inverse = norm_parts(tok[...].astype(f32))
    part, gain_grad[...] = norm_back(total[...], normed, inverse, gains[0:1, :])
    tokens_grad[...] = (middle_grad[...] + part).astype(bf16)


def grad_for_other(pairs, place, *refs):
    ins, out, flipped = refs[: 2 * pairs], refs[2 * pairs], refs[2 * pairs + 1]
    core = place[3]
    start = 0
    for i in range(pairs):
        x, dy = ins[2 * i], ins[2 * i + 1]
        half = dy.shape[1] // 2
        flipped[...] = x[...].T

        def step(t, _, dy=dy, half=half, start=start):
            made = dot(flipped[...], dy[:, columns((1 - core) * half + t * TILE, TILE)])
            out[:, columns(start + t * TILE, TILE)] = made.astype(bf16)
            return 0

        lax.fori_loop(0, half // TILE, step, 0)
        start += half


def grad_for_self(pairs, groups, place, *refs):
    ins, got, keep, send, natural, ordered = refs[: 2 * pairs], *refs[2 * pairs :]
    hb, core = place[1], place[3]
    high = keep.shape[1]
    cut = groups * high
    start = 0
    for i in range(pairs):
        x, dy = ins[2 * i], ins[2 * i + 1]
        half = dy.shape[1] // 2
        natural[...] = x[...].T
        for side in range(2):
            for g in range(groups):
                at = g * 2 * high + (hb ^ side) * high
                ordered[side * cut + g * high : side * cut + (g + 1) * high, :] = natural[rows(at, high), :]

        def step(t, _, dy=dy, half=half, start=start):
            made = dot(ordered[...], dy[:, columns(core * half + t * TILE, TILE)])
            out_at = columns(start + t * TILE, TILE)
            for side, target in enumerate((keep, send)):
                for g in range(groups):
                    at = g * 2 * high + (hb ^ side) * high
                    mine = made[side * cut + g * high : side * cut + (g + 1) * high, :]
                    target[g, :, out_at] = (mine + got[rows(at, high), out_at].astype(f32)).astype(bf16)
            return 0

        lax.fori_loop(0, half // TILE, step, 0)
        start += half


def add_split(groups, place, mine, got, keep, send):
    lb = place[2]
    low = keep.shape[1]
    step = mine.shape[1] - low
    for side, target in enumerate((keep, send)):
        at = rows((lb ^ side) * step, low)
        for g in range(groups):
            target[g] = (mine[g, at, :].astype(f32) + got[g, at, :].astype(f32)).astype(bf16)


def add_owners(groups, place, mine, got, *outs):
    z = place[0]
    for k in range(groups):
        g = lax.rem(z + k, groups)
        outs[k][...] = (mine[g].astype(f32) + got[g].astype(f32)).astype(outs[k].dtype)


def place_pieces(high, low, widths, place, *refs):
    parts, outs = refs[:8], refs[8:]
    hb, lb, core = place[1], place[2], place[3]
    size = parts[0].shape[0]
    for other in range(2):
        for flip_high in range(2):
            hi = (lb if other else hb) ^ flip_high
            lo = hb if other else lb
            one = parts[other * 4 + flip_high * 2]
            two = parts[other * 4 + flip_high * 2 + 1]
            start = 0
            for out, width in zip(outs, widths):
                at = columns((core ^ other) * width, width)
                a = one[:, start : start + width].astype(f32)
                b = two[:, start : start + width].astype(f32)
                out[rows(hi * high + low, size, 8), at] = jnp.where(lo == 0, b, a)
                out[rows(hi * high, size, 8), at] = jnp.where(lo == 0, a, b)
                start += width


def make(mesh):
    groups, copies = mesh.shape["group"], mesh.shape["replica"]
    swap_core = [(i, i ^ 1) for i in range(copies)]
    swap_two = [(i, i ^ 2) for i in range(copies)]
    swap_four = [(i, i ^ 4) for i in range(copies)]
    swap_high = [(i, i ^ (4 if i & 1 else 2)) for i in range(copies)]
    swap_low = [(i, i ^ (2 if i & 1 else 4)) for i in range(copies)]

    def across(a, perm):
        return lax.ppermute(a, "replica", perm)

    def shifted(a, k):
        return lax.ppermute(a, "group", [(i, (i + k) % groups) for i in range(groups)])

    def far_sum(a):
        if copies == 8:
            return a
        same = [[j + 8 * m for m in range(copies // 8)] for j in range(8)]
        return lax.psum(a, "replica", axis_index_groups=same)

    def spread(piece):
        a = jnp.stack([shifted(piece, k) for k in range(1, groups)])
        b = across(a, swap_high)
        c, d = across(a, swap_low), across(b, swap_low)
        here = [a, c, b, d]
        return here + [across(t, swap_core) for t in here], a

    def reduced(pairs, high, low, size, widths, place):
        flat = [t for pair in pairs for t in pair]
        depth, width = pairs[0][0].shape[1], sum(widths)
        length = pairs[0][0].shape[0]
        cost = 2 * length * depth * width
        turned = pltpu.VMEM((depth, length), bf16)
        (for_other,) = run(
            functools.partial(grad_for_other, len(pairs)), "grad_for_other",
            [shape((depth, width))], place, flat, [turned], cost,
        )
        got = across(for_other, swap_core)
        keep, send = run(
            functools.partial(grad_for_self, len(pairs), groups), "grad_for_self",
            [shape((groups, high, width))] * 2, place, flat + [got], [turned, turned], cost,
        )
        got = across(send, swap_high)
        keep, send = run(
            functools.partial(add_split, groups), "add_split",
            [shape((groups, size, width))] * 2, place, [keep, got],
        )
        got = across(send, swap_low)
        mine, *others = run(
            functools.partial(add_owners, groups), "add_owners",
            [shape((size, width), f32)] + [shape((size, width))] * (groups - 1), place, [keep, got],
        )
        for k, t in enumerate(others):
            mine = mine + shifted(t, k + 1).astype(f32)
        a = far_sum(mine).astype(bf16)
        c = across(a, swap_low)
        b, d = across(a, swap_high), across(c, swap_high)
        here = [a, c, b, d]
        parts = here + [across(t, swap_core) for t in here]
        return run(
            functools.partial(place_pieces, high, low, widths), "place_pieces",
            [shape((2 * high, 2 * w), f32) for w in widths], place, parts,
        )

    def on_device(tokens, segment, g_attn, w_qkv, w_out, g_mlp, w_in, w_down, grad_out):
        length = tokens.shape[0]
        z = lax.axis_index("group")
        r = lax.axis_index("replica")
        core, two, four = r & 1, (r >> 1) & 1, (r >> 2) & 1
        hb = jnp.where(core == 1, four, two)
        lb = jnp.where(core == 1, two, four)
        place = jnp.stack([z, hb, lb, core]).astype(jnp.int32)

        def cut(w, high, low, size):
            half = w.shape[1] // 2
            return lax.dynamic_slice(w, (high * hb + low * lb, half * core), (size, half))

        qkv_parts, ahead = spread(cut(w_qkv, 96, 48, 48))
        piece = jnp.concatenate([cut(w_in, 96, 48, 48), cut(w_out, 96, 48, 48)], axis=1)
        piece, _ = lax.optimization_barrier((piece, ahead))
        in_parts, ahead = spread(piece)
        piece, _ = lax.optimization_barrier((cut(w_down, 144, 64, 80), ahead))
        down_parts, _ = spread(piece)
        own_gains = jnp.stack([g_attn, g_mlp]).astype(f32)
        by_distance = jnp.stack([own_gains] + [shifted(own_gains, k) for k in range(1, groups)])
        gains = jnp.concatenate(
            [
                lax.dynamic_index_in_dim(by_distance, lax.rem(z + groups - g, groups), keepdims=False)
                for g in range(groups)
            ],
            axis=1,
        )
        cosine, sine = rotary_tables(token_positions(segment))
        seg_col, seg_row = segment[:, None], segment[None, :]

        attn_in, qkv, mixed, lse = run(
            functools.partial(attn_forward, groups), "attn_forward",
            [shape((length, D)), shape((length, 3 * D)), shape((length, D)), shape((length, PAIR), f32)],
            place, [tokens, gains, cosine, sine, seg_col, seg_row, w_qkv] + qkv_parts,
            [pltpu.VMEM((D, 3 * D), bf16)], 2 * length * D * 3 * D * 2,
        )
        middle, mlp_in, hidden, act, slope = run(
            functools.partial(mlp_forward, groups), "mlp_forward",
            [shape((length, D), f32), shape((length, D)), shape((length, FF)), shape((length, FF), f32), shape((length, FF), f32)],
            place, [tokens, mixed, gains, w_in, w_out] + in_parts,
            [pltpu.VMEM((D, 2 * FF), bf16), pltpu.VMEM((D, D), bf16)], 2 * length * D * (2 * FF + D),
        )

        (down_grad,) = reduced([(hidden, grad_out)], 144, 64, 80, [D // 2], place)
        output, gate_up_grad = run(
            functools.partial(down_backward, groups), "down_backward",
            [shape((length, D)), shape((length, 2 * FF))],
            place, [grad_out, hidden, middle, act, slope, w_down] + down_parts,
            [pltpu.VMEM((FF, D), bf16)], 4 * length * D * FF,
        )
        (in_grad,) = reduced([(mlp_in, gate_up_grad)], 96, 48, 48, [FF], place)
        middle_grad, branch_grad, mixed_grad, gain_two_grad = run(
            functools.partial(mlp_backward, groups), "mlp_backward",
            [shape((length, D), f32), shape((length, D)), shape((length, D)), shape((1, D), f32)],
            place, [gate_up_grad, grad_out, middle, gains, w_in, w_out] + in_parts,
            [pltpu.VMEM((D, 2 * FF), bf16), pltpu.VMEM((D, D), bf16), pltpu.VMEM((length, D), f32)],
            2 * length * D * (2 * FF + D),
        )
        (qkv_grad,) = run(
            attn_backward, "attn_backward", [shape((length, 3 * D))],
            place, [qkv, lse, mixed_grad, cosine, sine, seg_col, seg_row], (), 4 * length * D * 3 * D,
        )
        qkv_weight_grad, out_grad = reduced(
            [(attn_in, qkv_grad), (mixed, branch_grad)], 96, 48, 48, [3 * D // 2, D // 2], place
        )
        tokens_grad, gain_one_grad = run(
            functools.partial(attn_in_backward, groups), "attn_in_backward",
            [shape((length, D)), shape((1, D), f32)],
            place, [qkv_grad, tokens, middle_grad, gains, w_qkv] + qkv_parts,
            [pltpu.VMEM((D, 3 * D), bf16), pltpu.VMEM((length, D), f32)], 2 * length * D * 3 * D,
        )

        gain_grads = jnp.concatenate([gain_one_grad, gain_two_grad], axis=0)
        for perm in (swap_core, swap_two, swap_four):
            gain_grads = gain_grads + across(gain_grads, perm)
        gain_grads = far_sum(gain_grads)
        total = gain_grads
        for k in range(1, groups):
            total = total + shifted(gain_grads, k)
        shard = g_attn.shape[0]
        owned = lax.dynamic_slice(total, (0, z * shard), (2, shard))
        return (
            output, tokens_grad, owned[0], qkv_weight_grad, out_grad, owned[1], in_grad, down_grad,
        )

    return on_device


def solution(mesh):
    both = ("replica", "group")
    in_specs = (
        P(both, None), P(both), P("group"), P("group", None), P("group", None),
        P("group"), P("group", None), P("group", None), P(both, None),
    )
    out_specs = (
        P(both, None), P(both, None), P("group"), P("group", None),
        P("group", None), P("group"), P("group", None), P("group", None),
    )
    return jax.shard_map(
        make(mesh), mesh=mesh, in_specs=in_specs, out_specs=out_specs, check_vma=False
    )
```

```python
import functools

import jax
import jax.numpy as jnp
from jax import lax
from jax.experimental import pallas as pl
from jax.experimental.pallas import tpu as pltpu
from jax.sharding import PartitionSpec as P

HEADS = 12
HEAD_DIM = 64
FF = 1152
D = 768
TILE = 384
PAIR = 128
ROWS = 48
QKV = 3 * D // 2
IN_OUT = FF + D // 2
DOWN = 640
MLP = IN_OUT + DOWN

norm_eps = 1e-05
rope_base = 160000.0
head_scale = HEAD_DIM ** (-0.5)
f32 = jnp.float32
bf16 = jnp.bfloat16

VMEM = pl.BlockSpec(memory_space=pltpu.VMEM)
SMEM = pl.BlockSpec(memory_space=pltpu.SMEM)
ANY = pl.BlockSpec(memory_space=pl.ANY)


def run(body, name, outs, place, ins, scratch=(), after=()):
    count, extra = len(ins), len(after)

    def inner(place, *refs):
        body(place, *refs[:count], *refs[count + extra :])

    return pl.pallas_call(
        inner,
        out_shape=outs,
        in_specs=[SMEM] + [VMEM] * count + [ANY] * extra,
        out_specs=[VMEM] * len(outs),
        scratch_shapes=list(scratch),
        compiler_params=pltpu.CompilerParams(vmem_limit_bytes=44 * 1024 * 1024),
        cost_estimate=pl.CostEstimate(flops=0, bytes_accessed=0, transcendentals=0),
        name=name,
    )(place, *ins, *after)


def shape(dims, dtype=bf16):
    return jax.ShapeDtypeStruct(dims, dtype)


def dot(a, b):
    return lax.dot_general(a, b, (((1,), (0,)), ((), ())), preferred_element_type=f32)


def dot_bt(a, b):
    return lax.dot_general(a, b, (((1,), (1,)), ((), ())), preferred_element_type=f32)


def dot_at(a, b):
    return lax.dot_general(a, b, (((0,), (0,)), ((), ())), preferred_element_type=f32)


def token_positions(segment):
    length = segment.shape[0]
    index = jnp.arange(length, dtype=jnp.int32)
    before = jnp.concatenate([jnp.full((1,), -1, jnp.int32), segment[:-1]])
    first = lax.cummax(jnp.where(segment != before, index, 0), axis=0)
    return index - first


def rotary_tables(position):
    half_dim = HEAD_DIM // 2
    inverse = rope_base ** (-(jnp.arange(half_dim, dtype=f32) * 2.0 / HEAD_DIM))
    angles = position.astype(f32)[:, None] * inverse[None, :]
    cosine, sine = jnp.cos(angles), jnp.sin(angles)
    return (
        jnp.concatenate([cosine] * 4, axis=1),
        jnp.concatenate([-sine, sine, -sine, sine], axis=1),
    )


def rows(start, size, step=16):
    return pl.ds(pl.multiple_of(start, step), size)


def columns(start, size):
    return pl.ds(pl.multiple_of(start, 128), size)


def piece_rows(place, flip_high, flip_low, other):
    hb, lb = place[1], place[2]
    return (lb if other else hb) ^ flip_high, (hb if other else lb) ^ flip_low


def each_part(groups, place, parts):
    for index, part in enumerate(parts):
        flip_low, other = index & 1, index >> 1
        for flip_high in range(2):
            hi, lo = piece_rows(place, flip_high, flip_low, other)
            for k in range(1, groups):
                owner = lax.rem(place[0] + groups - k, groups)
                yield part, flip_high, k - 1, owner, hi, lo, place[3] ^ other


def assemble(groups, place, parts, own, full, width, start):
    shard = own.shape[0]
    full[rows(place[0] * shard, shard), :] = own[...]
    for part, i, j, owner, hi, lo, half in each_part(groups, place, parts):
        at = owner * shard + hi * 2 * ROWS + lo * ROWS
        full[rows(at, ROWS), columns(half * width, width)] = part[i, j, :, start : start + width]


def packed_blocks():
    for i in range(5):
        for j in range(3):
            n = 3 * i + j
            yield i, 16 * i, PAIR * j, 16 * (n % 3), PAIR * (n // 3)


def norm_parts(values):
    centred = values - jnp.mean(values, axis=1, keepdims=True)
    inverse = lax.rsqrt(jnp.mean(centred * centred, axis=1, keepdims=True) + norm_eps)
    return centred * inverse, inverse


def norm_back(upstream, normed, inverse, gain):
    scaled = upstream * gain
    inner = (
        scaled
        - jnp.mean(scaled, axis=1, keepdims=True)
        - normed * jnp.mean(scaled * normed, axis=1, keepdims=True)
    )
    return inverse * inner


def swap_halves(u):
    lane = lax.broadcasted_iota(jnp.int32, u.shape, 1)
    return jnp.where(lane % HEAD_DIM < HEAD_DIM // 2, pltpu.roll(u, PAIR - 32, 1), pltpu.roll(u, 32, 1))


def copy_half(place, whole, half):
    width = whole.shape[1] // 2
    half[...] = whole[:, columns((1 - place[3]) * width, width)]


def head_masks():
    lane = lax.broadcasted_iota(jnp.int32, (1, PAIR), 1)
    first = (lane < HEAD_DIM).astype(f32)
    return first.astype(bf16), (1.0 - first).astype(bf16)


def attn_forward(groups, place, gains, cosine, sine, seg_col, seg_row, tok, own, *rest):
    parts, (attn_in, qkv, mixed, lse, w_full) = rest[:4], rest[4:]
    assemble(groups, place, parts, own, w_full, QKV, 0)
    normed, _ = norm_parts(tok[...].astype(f32))
    attn_in[...] = (normed * gains[0:1, :]).astype(bf16)

    def turned(j, _):
        at = columns(j * TILE, TILE)
        raw = dot(attn_in[...], w_full[:, at])
        turned_parts = []
        for i in range(TILE // PAIR):
            u = raw[:, i * PAIR : (i + 1) * PAIR]
            turned_parts.append(u * cosine[...] + swap_halves(u) * sine[...])
        qkv[:, at] = jnp.concatenate(turned_parts, axis=1).astype(bf16)
        return 0

    lax.fori_loop(0, 4, turned, 0)

    def plain(j, _):
        at = columns(j * TILE, TILE)
        qkv[:, at] = dot(attn_in[...], w_full[:, at]).astype(bf16)
        return 0

    lax.fori_loop(4, 6, plain, 0)
    masks = head_masks()
    same = seg_col[...] == seg_row[...]
    length = tok.shape[0]
    lane = lax.broadcasted_iota(jnp.int32, (length, PAIR), 1)

    def pair(j, kept):
        q = qkv[:, columns(j * PAIR, PAIR)]
        k = qkv[:, columns(D + j * PAIR, PAIR)]
        v = qkv[:, columns(2 * D + j * PAIR, PAIR)]
        made = []
        for a in range(2):
            scores = dot_bt(q * masks[a], k) * head_scale
            scores = jnp.where(same, scores, -1e30)
            top = jnp.max(scores, axis=1, keepdims=True)
            e = jnp.exp(scores - top)
            total = jnp.sum(e, axis=1, keepdims=True)
            probs = (e * (1.0 / total)).astype(bf16)
            made.append(dot(probs, v))
            kept = jnp.where(lane == 2 * j + a, top + jnp.log(total), kept)
        mixed[:, columns(j * PAIR, PAIR)] = jnp.where(lane < HEAD_DIM, made[0], made[1]).astype(bf16)
        return kept

    lse[...] = lax.fori_loop(0, HEADS // 2, pair, jnp.zeros((length, PAIR), f32), unroll=2)


def feed_forward(groups, place, gains, mixed, attn_in, tok, grad_out, own_in, own_out, own_down, *rest):
    parts, rest = rest[:4], rest[4:]
    output, middle_grad, mixed_grad, branch_grad, hidden, mlp_in, gate_up_grad, for_other = rest[:8]
    w_in, w_out, w_down, middle, act, slope, total = rest[8:]
    assemble(groups, place, parts, own_out, w_out, D // 2, FF)
    assemble(groups, place, parts, own_in, w_in, FF, 0)
    shard = own_down.shape[0]
    w_down[rows(place[0] * shard, shard), :] = own_down[...]
    for part, i, j, owner, hi, lo, half in each_part(groups, place, parts):
        base = owner * shard + hi * 144 + lo * 64
        for _, r, c, pr, pc in packed_blocks():
            block = part[i, j, pr : pr + 16, IN_OUT + pc : IN_OUT + pc + PAIR]
            w_down[rows(base + r, 16), columns(half * (D // 2) + c, PAIR)] = block

    for j in range(2):
        at = slice(j * TILE, (j + 1) * TILE)
        middle[:, at] = tok[:, at].astype(f32) + dot(mixed[...], w_out[:, at])
    normed, inverse = norm_parts(middle[...])
    mlp_in[...] = (normed * gains[1:2, :]).astype(bf16)

    def forward(j, _):
        at = columns(j * TILE, TILE)
        u = dot(mlp_in[...], w_in[:, at])
        gate = dot(mlp_in[...], w_in[:, columns(FF + j * TILE, TILE)])
        cdf = 0.5 + 0.5 * lax.erf(u * 0.7071067811865476)
        a = u * cdf
        act[:, at] = a
        slope[:, at] = gate * (cdf + u * (0.3989422804014327 * jnp.exp(-0.5 * u * u)))
        hidden[:, at] = (a * gate).astype(bf16)
        return 0

    lax.fori_loop(0, FF // TILE, forward, 0)

    def backward(j, _):
        at = columns(j * TILE, TILE)
        hidden_grad = dot_bt(grad_out[...], w_down[rows(j * TILE, TILE), :])
        gate_up_grad[:, at] = (hidden_grad * slope[:, at]).astype(bf16)
        gate_up_grad[:, columns(FF + j * TILE, TILE)] = (hidden_grad * act[:, at]).astype(bf16)
        return 0

    lax.fori_loop(0, FF // TILE, backward, 0)
    for j in range(2):
        at = slice(j * TILE, (j + 1) * TILE)
        output[:, at] = (middle[:, at] + dot(hidden[...], w_down[:, at])).astype(bf16)

    def step(j, _):
        total[:, columns(j * 256, 256)] = dot_bt(gate_up_grad[...], w_in[rows(j * 256, 256), :])
        return 0

    lax.fori_loop(0, D // 256, step, 0)
    normed, inverse = norm_parts(middle[...])
    part = norm_back(total[...], normed, inverse, gains[1:2, :])
    whole = grad_out[...].astype(f32) + part
    middle_grad[...] = whole
    branch_grad[...] = whole.astype(bf16)

    def back(j, _):
        mixed_grad[:, columns(j * 256, 256)] = dot_bt(
            branch_grad[...], w_out[rows(j * 256, 256), :]
        ).astype(bf16)
        return 0

    lax.fori_loop(0, D // 256, back, 0)
    start = 0
    for whole in (hidden, mlp_in, mixed, attn_in):
        for_other[:, start : start + whole.shape[1]] = whole[...]
        start += whole.shape[1]
    for whole in (grad_out, gate_up_grad, branch_grad):
        width = whole.shape[1] // 2
        for_other[:, start : start + width] = whole[:, columns((1 - place[3]) * width, width)]
        start += width


HIDDEN, MLP_IN, MIXED, ATTN_IN, UPSTREAM, GATE_UP, BRANCH, SENT = (
    0, FF, FF + D, FF + 2 * D, FF + 3 * D, FF + 3 * D + D // 2, 2 * FF + 3 * D + D // 2, 2 * FF + 4 * D
)


def attn_backward(place, qkv, lse, mixed_grad, cosine, sine, seg_col, seg_row, qkv_grad, for_other):
    masks = head_masks()
    same = seg_col[...] == seg_row[...]
    length = qkv.shape[0]
    lane = lax.broadcasted_iota(jnp.int32, (length, PAIR), 1)

    def pair(j, _):
        q = qkv[:, columns(j * PAIR, PAIR)]
        k = qkv[:, columns(D + j * PAIR, PAIR)]
        v = qkv[:, columns(2 * D + j * PAIR, PAIR)]
        upstream = mixed_grad[:, columns(j * PAIR, PAIR)]
        made = []
        for a in range(2):
            scores = dot_bt(q * masks[a], k) * head_scale
            log_total = jnp.sum(jnp.where(lane == 2 * j + a, lse[...], 0.0), axis=1, keepdims=True)
            probs = jnp.where(same, jnp.exp(scores - log_total), 0.0)
            prob_grad = dot_bt(upstream * masks[a], v)
            delta = jnp.sum(probs * prob_grad, axis=1, keepdims=True)
            score_grad = (probs * (prob_grad - delta)).astype(bf16)
            made.append(
                (
                    dot(score_grad, k),
                    dot_at(score_grad, q),
                    dot_at(probs.astype(bf16), upstream),
                )
            )
        first = lane < HEAD_DIM
        for i in range(2):
            u = jnp.where(first, made[0][i], made[1][i]) * head_scale
            u = u * cosine[...] - swap_halves(u) * sine[...]
            qkv_grad[:, columns(i * D + j * PAIR, PAIR)] = u.astype(bf16)
        qkv_grad[:, columns(2 * D + j * PAIR, PAIR)] = jnp.where(first, made[0][2], made[1][2]).astype(bf16)
        return 0

    lax.fori_loop(0, HEADS // 2, pair, 0, unroll=2)
    copy_half(place, qkv_grad, for_other)


def attn_in_backward(groups, place, qkv_grad, middle_grad, gains, tok, own, *rest):
    parts, (tokens_grad, w_full, total) = rest[:4], rest[4:]
    assemble(groups, place, parts, own, w_full, QKV, 0)

    def step(j, _):
        total[:, columns(j * 256, 256)] = dot_bt(qkv_grad[...], w_full[rows(j * 256, 256), :])
        return 0

    lax.fori_loop(0, D // 256, step, 0)
    normed, inverse = norm_parts(tok[...].astype(f32))
    part = norm_back(total[...], normed, inverse, gains[0:1, :])
    tokens_grad[...] = (middle_grad[...] + part).astype(bf16)


def grad_for_self(plan, groups, place, *refs):
    ins, (keep, send, natural, ordered, right) = refs[:-5], refs[-5:]
    hb, core = place[1], place[3]
    high = keep.shape[1]
    cut = groups * high
    start = 0
    for x, (x_from, x_at), dy, (dy_from, dy_at) in plan:
        x, x_other, dy, dy_other = ins[x], ins[x_from], ins[dy], ins[dy_from]
        length, depth = x.shape
        half = dy.shape[1] // 2
        natural[:, :length] = x[...].T
        natural[:, length:] = x_other[:, x_at : x_at + depth].T
        for side in range(2):
            for g in range(groups):
                at = g * 2 * high + (hb ^ side) * high
                ordered[side * cut + g * high : side * cut + (g + 1) * high, :] = natural[rows(at, high), :]
        right[:length, :half] = dy[:, columns(core * half, half)]
        right[length:, :half] = dy_other[:, dy_at : dy_at + half]

        def step(t, _, start=start):
            made = dot(ordered[...], right[:, columns(t * TILE, TILE)])
            at = columns(start + t * TILE, TILE)
            for side, target in enumerate((keep, send)):
                for g in range(groups):
                    target[g, :, at] = made[side * cut + g * high : side * cut + (g + 1) * high, :].astype(bf16)
            return 0

        lax.fori_loop(0, half // TILE, step, 0)
        start += half


def split_mlp(groups, place, down, down_got, rest, rest_got, keep, send):
    lb = place[2]
    for side, target in enumerate((keep, send)):
        low, low_down = rows((lb ^ side) * ROWS, ROWS), rows((lb ^ side) * 64, 80)
        for g in range(groups):
            target[g, :, :IN_OUT] = (rest[g, low, :].astype(f32) + rest_got[g, low, :].astype(f32)).astype(bf16)
            made = (down[g, low_down, :].astype(f32) + down_got[g, low_down, :].astype(f32)).astype(bf16)
            for _, r, c, pr, pc in packed_blocks():
                target[g, pr : pr + 16, IN_OUT + pc : IN_OUT + pc + PAIR] = made[r : r + 16, c : c + PAIR]


def split_qkv(groups, place, mine, got, keep, send):
    for side, target in enumerate((keep, send)):
        low = rows((place[2] ^ side) * ROWS, ROWS)
        for g in range(groups):
            target[g] = (mine[g, low, :].astype(f32) + got[g, low, :].astype(f32)).astype(bf16)


def add_owners(groups, place, mine, got, *outs):
    for k in range(groups):
        g = lax.rem(place[0] + k, groups)
        outs[k][...] = (mine[g].astype(f32) + got[g].astype(f32)).astype(outs[k].dtype)


def sum_pieces(groups, place, mine, *refs):
    total = mine[...]
    for ref in refs[:-1]:
        total = total + ref[...].astype(f32)
    refs[-1][...] = total.astype(refs[-1].dtype)


def gain_grad(grad, weight, gain):
    return jnp.sum(grad * weight.astype(f32), axis=1, keepdims=True) / gain


def place_mlp(place, gain, here, other, weight, in_grad, out_grad, down_grad, gain_out):
    for core, part in enumerate((here, other)):
        for flip_high in range(2):
            hi, lo = piece_rows(place, flip_high, 0, core)
            half = place[3] ^ core
            for flip_low in range(2):
                at = rows(hi * 2 * ROWS + (lo ^ flip_low) * ROWS, ROWS)
                piece = part[flip_high, flip_low]
                in_grad[at, columns(half * FF, FF)] = piece[:, :FF].astype(f32)
                out_grad[at, columns(half * (D // 2), D // 2)] = piece[:, FF:IN_OUT].astype(f32)
            one = part[flip_high, 0, :, IN_OUT:].astype(f32)
            two = part[flip_high, 1, :, IN_OUT:].astype(f32)
            low, up = jnp.where(lo == 0, one, two), jnp.where(lo == 0, two, one)
            for i, r, c, pr, pc in packed_blocks():
                at = columns(half * (D // 2) + c, PAIR)
                down_grad[rows(hi * 144 + r, 16), at] = low[pr : pr + 16, pc : pc + PAIR]
                if i > 0:
                    down_grad[rows(hi * 144 + 64 + r, 16), at] = up[pr : pr + 16, pc : pc + PAIR]
    gain_out[...] = gain_grad(in_grad[...], weight[...], gain[...])


def place_qkv(place, gain, here, other, weight, grad, gain_out):
    for core, part in enumerate((here, other)):
        for flip_high in range(2):
            for flip_low in range(2):
                hi, lo = piece_rows(place, flip_high, flip_low, core)
                at = rows(hi * 2 * ROWS + lo * ROWS, ROWS)
                grad[at, columns((place[3] ^ core) * QKV, QKV)] = part[flip_high, flip_low].astype(f32)
    gain_out[...] = gain_grad(grad[...], weight[...], gain[...])


def stack_pieces(count, place, *refs):
    for k, ref in enumerate(refs[:count]):
        start = 0
        for out in refs[count:]:
            width = out.shape[2]
            out[k] = ref[:, start : start + width]
            start += width


def join(place, near, got, out):
    out[0] = near[...]
    out[1] = got[...]


def make(mesh):
    groups, copies = mesh.shape["group"], mesh.shape["replica"]
    swap_core = [(i, i ^ 1) for i in range(copies)]
    swap_high = [(i, i ^ (4 if i & 1 else 2)) for i in range(copies)]
    swap_low = [(i, i ^ (2 if i & 1 else 4)) for i in range(copies)]
    far_same = [[j + 8 * m for m in range(copies // 8)] for j in range(8)]

    def across(a, perm):
        return lax.ppermute(a, "replica", perm)

    def shifted(a, k):
        return lax.ppermute(a, "group", [(i, (i + k) % groups) for i in range(groups)])

    def on_device(tokens, segment, g_attn, w_qkv, w_out, g_mlp, w_in, w_down, grad_out):
        length = tokens.shape[0]
        z = lax.axis_index("group")
        r = lax.axis_index("replica")
        core, two, four = r & 1, (r >> 1) & 1, (r >> 2) & 1
        hb = jnp.where(core == 1, four, two)
        lb = jnp.where(core == 1, two, four)
        place = jnp.stack([z, hb, lb, core]).astype(jnp.int32)

        def joined(near, got, after=()):
            return run(join, "join", [shape((2,) + near.shape)], place, [near, got], (), after)[0]

        def spread(a, after=()):
            here = joined(a, across(a, swap_high), after)
            low = across(here, swap_low)
            return [here, low, across(here, swap_core), across(low, swap_core)]

        def grad_self(ins, plan, high, after=()):
            depth = ins[plan[0][0]].shape[1]
            widths = [ins[dy].shape[1] // 2 for _, _, dy, _ in plan]
            turned = pltpu.VMEM((depth, 2 * length), bf16)
            keep, send = run(
                functools.partial(grad_for_self, plan, groups), "grad_for_self",
                [shape((groups, high, sum(widths)))] * 2, place, ins,
                [turned, turned, pltpu.VMEM((2 * length, max(widths)), bf16)], after,
            )
            return keep, across(send, swap_high)

        def owners(keep, got, after=()):
            dims = keep.shape[1:]
            mine, *others = run(
                functools.partial(add_owners, groups), "add_owners",
                [shape(dims, f32)] + [shape(dims)] * (groups - 1), place, [keep, got],
                (), after,
            )
            return mine, [shifted(t, k + 1) for k, t in enumerate(others)]

        def summed(mine, got, after=()):
            kind = bf16 if copies == 8 else f32
            (total,) = run(
                functools.partial(sum_pieces, groups), "sum_pieces", [shape(mine.shape, kind)], place,
                [mine] + list(got), (), after,
            )
            if copies > 8:
                total = lax.psum(total, "replica", axis_index_groups=far_same).astype(bf16)
            return total

        count = 2 * g_attn.shape[0] // PAIR
        own_gains = jnp.pad(jnp.concatenate([g_attn, g_mlp]).reshape(count, PAIR), ((0, ROWS - count), (0, 0)))

        def cut(w, at, size):
            half = w.shape[1] // 2
            return lax.dynamic_slice(w, (at, half * core), (size, half))

        quarter = 2 * ROWS * hb + ROWS * lb
        qkv_piece = jnp.concatenate([cut(w_qkv, quarter, ROWS), own_gains], axis=1)
        down = cut(w_down, 144 * hb + 64 * lb, 80).reshape(5, 16, 3, PAIR).transpose(2, 1, 0, 3).reshape(ROWS, DOWN)
        mlp_piece = jnp.concatenate([cut(w_in, quarter, ROWS), cut(w_out, quarter, ROWS), down], axis=1)
        cosine, sine = rotary_tables(token_positions(segment))
        seg_col, seg_row = segment[:, None], segment[None, :]
        qkv_stack, far_gains = run(
            functools.partial(stack_pieces, groups - 1), "stack_pieces", [shape((groups - 1, ROWS, QKV)), shape((groups - 1, ROWS, PAIR))], place,
            [shifted(qkv_piece, k) for k in range(1, groups)], (), [cosine, sine],
        )
        mlp_far = [shifted(mlp_piece, k) for k in range(1, groups)]
        qkv_parts = spread(qkv_stack, mlp_far[:1])
        (mlp_stack,) = run(
            functools.partial(stack_pieces, groups - 1), "stack_pieces", [shape((groups - 1, ROWS, MLP))], place,
            list(mlp_far), (), qkv_parts[1:3],
        )
        by_distance = jnp.concatenate([own_gains[None], far_gains])[:, :count]
        by_distance = by_distance.reshape(groups, 2, g_attn.shape[0]).astype(f32)
        gains = jnp.concatenate(
            [
                lax.dynamic_index_in_dim(by_distance, lax.rem(z + groups - g, groups), keepdims=False)
                for g in range(groups)
            ],
            axis=1,
        )

        rope = [cosine, sine, seg_col, seg_row]
        attn_in, qkv, mixed, lse = run(
            functools.partial(attn_forward, groups), "attn_forward",
            [shape((length, D)), shape((length, 3 * D)), shape((length, D)), shape((length, PAIR), f32)],
            place, [gains] + rope + [tokens, w_qkv] + qkv_parts,
            [pltpu.VMEM((D, 3 * D), bf16)], [mlp_stack],
        )
        mlp_parts = spread(mlp_stack, [mixed])
        output, middle_grad, mixed_grad, branch_grad, hidden, mlp_in, gate_up_grad, for_other = run(
            functools.partial(feed_forward, groups), "feed_forward",
            [
                shape((length, D)), shape((length, D), f32), shape((length, D)), shape((length, D)),
                shape((length, FF)), shape((length, D)), shape((length, 2 * FF)), shape((length, SENT)),
            ],
            place, [gains, mixed, attn_in, tokens, grad_out, w_in, w_out, w_down] + mlp_parts,
            [
                pltpu.VMEM((D, 2 * FF), bf16), pltpu.VMEM((D, D), bf16), pltpu.VMEM((FF, D), bf16),
                pltpu.VMEM((length, D), f32), pltpu.VMEM((length, FF), f32), pltpu.VMEM((length, FF), f32),
                pltpu.VMEM((length, D), f32),
            ],
        )
        from_other = across(for_other, swap_core)

        qkv_grad, qkv_send = run(
            attn_backward, "attn_backward", [shape((length, 3 * D)), shape((length, QKV))],
            place, [qkv, lse, mixed_grad] + rope,
        )
        qkv_other = across(qkv_send, swap_core)
        down_keep, down_got = grad_self(
            [hidden, grad_out, from_other], [(0, (2, HIDDEN), 1, (2, UPSTREAM))], 144, [qkv_send]
        )
        rest_keep, rest_got = grad_self(
            [mlp_in, gate_up_grad, mixed, branch_grad, from_other],
            [(0, (4, MLP_IN), 1, (4, GATE_UP)), (2, (4, MIXED), 3, (4, BRANCH))], 96, [down_keep],
        )
        qkv_keep, qkv_got = grad_self(
            [attn_in, qkv_grad, from_other, qkv_other], [(0, (2, ATTN_IN), 1, (3, 0))], 96, [rest_keep]
        )
        mlp_keep, mlp_send = run(
            functools.partial(split_mlp, groups), "split_mlp", [shape((groups, ROWS, MLP))] * 2, place,
            [down_keep, down_got, rest_keep, rest_got],
            (), [qkv_keep],
        )
        mlp_got = across(mlp_send, swap_low)
        (tokens_grad,) = run(
            functools.partial(attn_in_backward, groups), "attn_in_backward", [shape((length, D))],
            place, [qkv_grad, middle_grad, gains] + [tokens, w_qkv] + qkv_parts,
            [pltpu.VMEM((D, 3 * D), bf16), pltpu.VMEM((length, D), f32)], [mlp_keep],
        )
        qkv_keep, qkv_send = run(
            functools.partial(split_qkv, groups), "split_qkv", [shape((groups, ROWS, QKV))] * 2, place,
            [qkv_keep, qkv_got], (), [tokens_grad],
        )
        qkv_got = across(qkv_send, swap_low)
        mlp_mine, mlp_others = owners(mlp_keep, mlp_got, [qkv_keep])
        qkv_mine, qkv_others = owners(qkv_keep, qkv_got, [mlp_mine])
        mlp_sum = summed(mlp_mine, mlp_others, [qkv_mine])
        mlp_pair = joined(mlp_sum, across(mlp_sum, swap_low))
        qkv_sum = summed(qkv_mine, qkv_others, [mlp_pair])
        mlp_quarters = joined(mlp_pair, across(mlp_pair, swap_high), [qkv_sum])
        qkv_pair = joined(qkv_sum, across(qkv_sum, swap_low), [mlp_quarters])
        qkv_quarters = joined(qkv_pair, across(qkv_pair, swap_high))
        shard = w_in.shape[0]
        in_grad, out_grad, down_grad, gain_two_grad = run(
            place_mlp, "place_mlp",
            [shape((shard, 2 * FF), f32), shape((shard, D), f32), shape((w_down.shape[0], D), f32), shape((shard, 1), f32)],
            place, [g_mlp.astype(f32)[:, None], mlp_quarters, across(mlp_quarters, swap_core), w_in],
            (), [qkv_pair],
        )
        qkv_weight_grad, gain_one_grad = run(
            place_qkv, "place_qkv", [shape((shard, 3 * D), f32), shape((shard, 1), f32)], place,
            [g_attn.astype(f32)[:, None], qkv_quarters, across(qkv_quarters, swap_core), w_qkv],
            (), [in_grad],
        )
        return (
            output, tokens_grad, gain_one_grad[:, 0], qkv_weight_grad, out_grad, gain_two_grad[:, 0], in_grad, down_grad,
        )

    return on_device


def solution(mesh):
    both = ("replica", "group")
    in_specs = (
        P(both, None), P(both), P("group"), P("group", None), P("group", None),
        P("group"), P("group", None), P("group", None), P(both, None),
    )
    out_specs = (
        P(both, None), P(both, None), P("group"), P("group", None),
        P("group", None), P("group"), P("group", None), P("group", None),
    )
    return jax.shard_map(
        make(mesh), mesh=mesh, in_specs=in_specs, out_specs=out_specs, check_vma=False
    )
```

```python
import functools

import jax
import jax.numpy as jnp
from jax import lax
from jax.experimental import pallas as pl
from jax.experimental.pallas import tpu as pltpu
from jax.sharding import PartitionSpec as P

HEADS = 12
HEAD_DIM = 64
FF = 1152
D = 768
TILE = 384
PAIR = 128
ROWS = 48
QKV = 3 * D // 2
IN_OUT = FF + D // 2
DOWN = 640
MLP = IN_OUT + DOWN

norm_eps = 1e-05
rope_base = 160000.0
head_scale = HEAD_DIM ** (-0.5)
f32 = jnp.float32
bf16 = jnp.bfloat16

VMEM = pl.BlockSpec(memory_space=pltpu.VMEM)
SMEM = pl.BlockSpec(memory_space=pltpu.SMEM)
ANY = pl.BlockSpec(memory_space=pl.ANY)


def run(body, name, outs, place, ins, scratch=(), after=()):
    count, extra = len(ins), len(after)

    def inner(place, *refs):
        body(place, *refs[:count], *refs[count + extra :])

    return pl.pallas_call(
        inner,
        out_shape=outs,
        in_specs=[SMEM] + [VMEM] * count + [ANY] * extra,
        out_specs=[VMEM] * len(outs),
        scratch_shapes=list(scratch),
        compiler_params=pltpu.CompilerParams(vmem_limit_bytes=44 * 1024 * 1024),
        cost_estimate=pl.CostEstimate(flops=0, bytes_accessed=0, transcendentals=0),
        name=name,
    )(place, *ins, *after)


def shape(dims, dtype=bf16):
    return jax.ShapeDtypeStruct(dims, dtype)


def dot(a, b):
    return lax.dot_general(a, b, (((1,), (0,)), ((), ())), preferred_element_type=f32)


def dot_bt(a, b):
    return lax.dot_general(a, b, (((1,), (1,)), ((), ())), preferred_element_type=f32)


def dot_at(a, b):
    return lax.dot_general(a, b, (((0,), (0,)), ((), ())), preferred_element_type=f32)


def token_positions(segment):
    length = segment.shape[0]
    index = jnp.arange(length, dtype=jnp.int32)
    before = jnp.concatenate([jnp.full((1,), -1, jnp.int32), segment[:-1]])
    first = lax.cummax(jnp.where(segment != before, index, 0), axis=0)
    return index - first


def rotary_tables(position):
    half_dim = HEAD_DIM // 2
    inverse = rope_base ** (-(jnp.arange(half_dim, dtype=f32) * 2.0 / HEAD_DIM))
    angles = position.astype(f32)[:, None] * inverse[None, :]
    cosine, sine = jnp.cos(angles), jnp.sin(angles)
    return (
        jnp.concatenate([cosine] * 4, axis=1),
        jnp.concatenate([-sine, sine, -sine, sine], axis=1),
    )


def rows(start, size, step=16):
    return pl.ds(pl.multiple_of(start, step), size)


def columns(start, size):
    return pl.ds(pl.multiple_of(start, 128), size)


def piece_rows(place, flip_high, flip_low, other):
    hb, lb = place[1], place[2]
    return (lb if other else hb) ^ flip_high, (hb if other else lb) ^ flip_low


def each_part(groups, place, parts):
    for index, part in enumerate(parts):
        flip_low, other = index & 1, index >> 1
        for flip_high in range(2):
            hi, lo = piece_rows(place, flip_high, flip_low, other)
            for k in range(1, groups):
                owner = lax.rem(place[0] + groups - k, groups)
                yield part, flip_high, k - 1, owner, hi, lo, place[3] ^ other


def assemble(groups, place, parts, own, full, width, start):
    shard = own.shape[0]
    full[rows(place[0] * shard, shard), :] = own[...]
    for part, i, j, owner, hi, lo, half in each_part(groups, place, parts):
        at = owner * shard + hi * 2 * ROWS + lo * ROWS
        full[rows(at, ROWS), columns(half * width, width)] = part[i, j, :, start : start + width]


def packed_blocks():
    for i in range(5):
        for j in range(3):
            n = 3 * i + j
            yield i, 16 * i, PAIR * j, 16 * (n % 3), PAIR * (n // 3)


def norm_parts(values):
    centred = values - jnp.mean(values, axis=1, keepdims=True)
    inverse = lax.rsqrt(jnp.mean(centred * centred, axis=1, keepdims=True) + norm_eps)
    return centred * inverse, inverse


def norm_back(upstream, normed, inverse, gain):
    scaled = upstream * gain
    inner = (
        scaled
        - jnp.mean(scaled, axis=1, keepdims=True)
        - normed * jnp.mean(scaled * normed, axis=1, keepdims=True)
    )
    return inverse * inner


def swap_halves(u):
    lane = lax.broadcasted_iota(jnp.int32, u.shape, 1)
    return jnp.where(lane % HEAD_DIM < HEAD_DIM // 2, pltpu.roll(u, PAIR - 32, 1), pltpu.roll(u, 32, 1))


def copy_half(place, whole, half):
    width = whole.shape[1] // 2
    half[...] = whole[:, columns((1 - place[3]) * width, width)]


def head_masks():
    lane = lax.broadcasted_iota(jnp.int32, (1, PAIR), 1)
    first = (lane < HEAD_DIM).astype(f32)
    return first.astype(bf16), (1.0 - first).astype(bf16)


def attn_forward(groups, place, gains, cosine, sine, seg_col, seg_row, tok, own, *rest):
    parts, (attn_in, qkv, mixed, lse, for_other, w_full) = rest[:4], rest[4:]
    assemble(groups, place, parts, own, w_full, QKV, 0)
    normed, _ = norm_parts(tok[...].astype(f32))
    attn_in[...] = (normed * gains[0:1, :]).astype(bf16)

    def turned(j, _):
        at = columns(j * TILE, TILE)
        raw = dot(attn_in[...], w_full[:, at])
        turned_parts = []
        for i in range(TILE // PAIR):
            u = raw[:, i * PAIR : (i + 1) * PAIR]
            turned_parts.append(u * cosine[...] + swap_halves(u) * sine[...])
        qkv[:, at] = jnp.concatenate(turned_parts, axis=1).astype(bf16)
        return 0

    lax.fori_loop(0, 4, turned, 0)

    def plain(j, _):
        at = columns(j * TILE, TILE)
        qkv[:, at] = dot(attn_in[...], w_full[:, at]).astype(bf16)
        return 0

    lax.fori_loop(4, 6, plain, 0)
    masks = head_masks()
    same = seg_col[...] == seg_row[...]
    length = tok.shape[0]
    lane = lax.broadcasted_iota(jnp.int32, (length, PAIR), 1)

    def pair(j, kept):
        q = qkv[:, columns(j * PAIR, PAIR)]
        k = qkv[:, columns(D + j * PAIR, PAIR)]
        v = qkv[:, columns(2 * D + j * PAIR, PAIR)]
        made = []
        for a in range(2):
            scores = dot_bt(q * masks[a], k) * head_scale
            scores = jnp.where(same, scores, -1e30)
            top = jnp.max(scores, axis=1, keepdims=True)
            e = jnp.exp(scores - top)
            total = jnp.sum(e, axis=1, keepdims=True)
            probs = (e * (1.0 / total)).astype(bf16)
            made.append(dot(probs, v))
            kept = jnp.where(lane == 2 * j + a, top + jnp.log(total), kept)
        mixed[:, columns(j * PAIR, PAIR)] = jnp.where(lane < HEAD_DIM, made[0], made[1]).astype(bf16)
        return kept

    lse[...] = lax.fori_loop(0, HEADS // 2, pair, jnp.zeros((length, PAIR), f32), unroll=2)
    for_other[:, :D] = attn_in[...]
    for_other[:, D:] = mixed[...]


def feed_forward(groups, place, gains, mixed, tok, grad_out, own_in, own_out, own_down, *rest):
    parts, rest = rest[:4], rest[4:]
    output, middle_grad, mixed_grad, branch_grad, hidden, mlp_in, gate_up_grad, for_other = rest[:8]
    w_in, w_out, w_down, middle, act, slope, total = rest[8:]
    assemble(groups, place, parts, own_out, w_out, D // 2, FF)
    assemble(groups, place, parts, own_in, w_in, FF, 0)
    shard = own_down.shape[0]
    w_down[rows(place[0] * shard, shard), :] = own_down[...]
    for part, i, j, owner, hi, lo, half in each_part(groups, place, parts):
        base = owner * shard + hi * 144 + lo * 64
        for _, r, c, pr, pc in packed_blocks():
            block = part[i, j, pr : pr + 16, IN_OUT + pc : IN_OUT + pc + PAIR]
            w_down[rows(base + r, 16), columns(half * (D // 2) + c, PAIR)] = block

    for j in range(2):
        at = slice(j * TILE, (j + 1) * TILE)
        middle[:, at] = tok[:, at].astype(f32) + dot(mixed[...], w_out[:, at])
    normed, inverse = norm_parts(middle[...])
    mlp_in[...] = (normed * gains[1:2, :]).astype(bf16)

    def forward(j, _):
        at = columns(j * TILE, TILE)
        u = dot(mlp_in[...], w_in[:, at])
        gate = dot(mlp_in[...], w_in[:, columns(FF + j * TILE, TILE)])
        cdf = 0.5 + 0.5 * lax.erf(u * 0.7071067811865476)
        a = u * cdf
        act[:, at] = a
        slope[:, at] = gate * (cdf + u * (0.3989422804014327 * jnp.exp(-0.5 * u * u)))
        hidden[:, at] = (a * gate).astype(bf16)
        return 0

    lax.fori_loop(0, FF // TILE, forward, 0)

    def backward(j, _):
        at = columns(j * TILE, TILE)
        hidden_grad = dot_bt(grad_out[...], w_down[rows(j * TILE, TILE), :])
        gate_up_grad[:, at] = (hidden_grad * slope[:, at]).astype(bf16)
        gate_up_grad[:, columns(FF + j * TILE, TILE)] = (hidden_grad * act[:, at]).astype(bf16)
        return 0

    lax.fori_loop(0, FF // TILE, backward, 0)
    for j in range(2):
        at = slice(j * TILE, (j + 1) * TILE)
        output[:, at] = (middle[:, at] + dot(hidden[...], w_down[:, at])).astype(bf16)

    def step(j, _):
        total[:, columns(j * 256, 256)] = dot_bt(gate_up_grad[...], w_in[rows(j * 256, 256), :])
        return 0

    lax.fori_loop(0, D // 256, step, 0)
    normed, inverse = norm_parts(middle[...])
    part = norm_back(total[...], normed, inverse, gains[1:2, :])
    whole = grad_out[...].astype(f32) + part
    middle_grad[...] = whole
    branch_grad[...] = whole.astype(bf16)

    def back(j, _):
        mixed_grad[:, columns(j * 256, 256)] = dot_bt(
            branch_grad[...], w_out[rows(j * 256, 256), :]
        ).astype(bf16)
        return 0

    lax.fori_loop(0, D // 256, back, 0)
    start = 0
    for whole in (hidden, mlp_in):
        for_other[:, start : start + whole.shape[1]] = whole[...]
        start += whole.shape[1]
    for whole in (grad_out, gate_up_grad, branch_grad):
        width = whole.shape[1] // 2
        for_other[:, start : start + width] = whole[:, columns((1 - place[3]) * width, width)]
        start += width


HIDDEN, MLP_IN, UPSTREAM, GATE_UP, BRANCH, SENT = (
    0, FF, FF + D, FF + D + D // 2, 2 * FF + D + D // 2, 2 * FF + 2 * D
)


def attn_backward(place, qkv, lse, mixed_grad, cosine, sine, seg_col, seg_row, qkv_grad, for_other):
    masks = head_masks()
    same = seg_col[...] == seg_row[...]
    length = qkv.shape[0]
    lane = lax.broadcasted_iota(jnp.int32, (length, PAIR), 1)

    def pair(j, _):
        q = qkv[:, columns(j * PAIR, PAIR)]
        k = qkv[:, columns(D + j * PAIR, PAIR)]
        v = qkv[:, columns(2 * D + j * PAIR, PAIR)]
        upstream = mixed_grad[:, columns(j * PAIR, PAIR)]
        made = []
        for a in range(2):
            scores = dot_bt(q * masks[a], k) * head_scale
            log_total = jnp.sum(jnp.where(lane == 2 * j + a, lse[...], 0.0), axis=1, keepdims=True)
            probs = jnp.where(same, jnp.exp(scores - log_total), 0.0)
            prob_grad = dot_bt(upstream * masks[a], v)
            delta = jnp.sum(probs * prob_grad, axis=1, keepdims=True)
            score_grad = (probs * (prob_grad - delta)).astype(bf16)
            made.append(
                (
                    dot(score_grad, k),
                    dot_at(score_grad, q),
                    dot_at(probs.astype(bf16), upstream),
                )
            )
        first = lane < HEAD_DIM
        for i in range(2):
            u = jnp.where(first, made[0][i], made[1][i]) * head_scale
            u = u * cosine[...] - swap_halves(u) * sine[...]
            qkv_grad[:, columns(i * D + j * PAIR, PAIR)] = u.astype(bf16)
        qkv_grad[:, columns(2 * D + j * PAIR, PAIR)] = jnp.where(first, made[0][2], made[1][2]).astype(bf16)
        return 0

    lax.fori_loop(0, HEADS // 2, pair, 0, unroll=2)
    copy_half(place, qkv_grad, for_other)


def attn_in_backward(groups, place, qkv_grad, middle_grad, gains, tok, own, *rest):
    parts, (tokens_grad, w_full, total) = rest[:4], rest[4:]
    assemble(groups, place, parts, own, w_full, QKV, 0)

    def step(j, _):
        total[:, columns(j * 256, 256)] = dot_bt(qkv_grad[...], w_full[rows(j * 256, 256), :])
        return 0

    lax.fori_loop(0, D // 256, step, 0)
    normed, inverse = norm_parts(tok[...].astype(f32))
    part = norm_back(total[...], normed, inverse, gains[0:1, :])
    tokens_grad[...] = (middle_grad[...] + part).astype(bf16)


def grad_for_self(plan, groups, place, *refs):
    ins, (keep, send, natural, ordered, right) = refs[:-5], refs[-5:]
    hb, core = place[1], place[3]
    high = keep.shape[1]
    cut = groups * high
    start = 0
    for x, (x_from, x_at), dy, (dy_from, dy_at) in plan:
        x, x_other, dy, dy_other = ins[x], ins[x_from], ins[dy], ins[dy_from]
        length, depth = x.shape
        half = dy.shape[1] // 2
        natural[:, :length] = x[...].T
        natural[:, length:] = x_other[:, x_at : x_at + depth].T
        for side in range(2):
            for g in range(groups):
                at = g * 2 * high + (hb ^ side) * high
                ordered[side * cut + g * high : side * cut + (g + 1) * high, :] = natural[rows(at, high), :]
        right[:length, :half] = dy[:, columns(core * half, half)]
        right[length:, :half] = dy_other[:, dy_at : dy_at + half]

        def step(t, _, start=start):
            made = dot(ordered[...], right[:, columns(t * TILE, TILE)])
            at = columns(start + t * TILE, TILE)
            for side, target in enumerate((keep, send)):
                for g in range(groups):
                    target[g, :, at] = made[side * cut + g * high : side * cut + (g + 1) * high, :].astype(bf16)
            return 0

        lax.fori_loop(0, half // TILE, step, 0)
        start += half


def split_mlp(groups, place, down, down_got, rest, rest_got, keep, send):
    lb = place[2]
    for side, target in enumerate((keep, send)):
        low, low_down = rows((lb ^ side) * ROWS, ROWS), rows((lb ^ side) * 64, 80)
        for g in range(groups):
            target[g, :, :IN_OUT] = (rest[g, low, :].astype(f32) + rest_got[g, low, :].astype(f32)).astype(bf16)
            made = (down[g, low_down, :].astype(f32) + down_got[g, low_down, :].astype(f32)).astype(bf16)
            for _, r, c, pr, pc in packed_blocks():
                target[g, pr : pr + 16, IN_OUT + pc : IN_OUT + pc + PAIR] = made[r : r + 16, c : c + PAIR]


def split_qkv(groups, place, mine, got, keep, send):
    for side, target in enumerate((keep, send)):
        low = rows((place[2] ^ side) * ROWS, ROWS)
        for g in range(groups):
            target[g] = (mine[g, low, :].astype(f32) + got[g, low, :].astype(f32)).astype(bf16)


def add_owners(groups, place, mine, got, *outs):
    for k in range(groups):
        g = lax.rem(place[0] + k, groups)
        outs[k][...] = (mine[g].astype(f32) + got[g].astype(f32)).astype(outs[k].dtype)


def sum_pieces(groups, place, mine, *refs):
    total = mine[...]
    for ref in refs[:-1]:
        total = total + ref[...].astype(f32)
    refs[-1][...] = total.astype(refs[-1].dtype)


def gain_grad(grad, weight, gain):
    ones = jnp.ones((8, grad.shape[1]), f32)
    summed = lax.dot_general(
        ones, grad * weight.astype(f32), (((1,), (1,)), ((), ())),
        precision=lax.Precision.HIGHEST, preferred_element_type=f32,
    )
    return summed[0:1, :] / gain


def place_mlp(place, gain, here, other, weight, in_grad, out_grad, down_grad, gain_out):
    for core, part in enumerate((here, other)):
        for flip_high in range(2):
            hi, lo = piece_rows(place, flip_high, 0, core)
            half = place[3] ^ core
            for flip_low in range(2):
                at = rows(hi * 2 * ROWS + (lo ^ flip_low) * ROWS, ROWS)
                piece = part[flip_high, flip_low]
                in_grad[at, columns(half * FF, FF)] = piece[:, :FF].astype(f32)
                out_grad[at, columns(half * (D // 2), D // 2)] = piece[:, FF:IN_OUT].astype(f32)
            one = part[flip_high, 0, :, IN_OUT:].astype(f32)
            two = part[flip_high, 1, :, IN_OUT:].astype(f32)
            low, up = jnp.where(lo == 0, one, two), jnp.where(lo == 0, two, one)
            for i, r, c, pr, pc in packed_blocks():
                at = columns(half * (D // 2) + c, PAIR)
                down_grad[rows(hi * 144 + r, 16), at] = low[pr : pr + 16, pc : pc + PAIR]
                if i > 0:
                    down_grad[rows(hi * 144 + 64 + r, 16), at] = up[pr : pr + 16, pc : pc + PAIR]
    gain_out[...] = gain_grad(in_grad[...], weight[...], gain[...])


def place_qkv(place, gain, here, other, weight, grad, gain_out):
    for core, part in enumerate((here, other)):
        for flip_high in range(2):
            for flip_low in range(2):
                hi, lo = piece_rows(place, flip_high, flip_low, core)
                at = rows(hi * 2 * ROWS + lo * ROWS, ROWS)
                grad[at, columns((place[3] ^ core) * QKV, QKV)] = part[flip_high, flip_low].astype(f32)
    gain_out[...] = gain_grad(grad[...], weight[...], gain[...])


def stack_pieces(count, place, *refs):
    for k, ref in enumerate(refs[:count]):
        start = 0
        for out in refs[count:]:
            width = out.shape[2]
            out[k] = ref[:, start : start + width]
            start += width


def keep_copy(place, given, out):
    out[...] = given[...]


def join(place, near, got, out):
    out[0] = near[...]
    out[1] = got[...]


def make(mesh):
    groups, copies = mesh.shape["group"], mesh.shape["replica"]
    swap_core = [(i, i ^ 1) for i in range(copies)]
    swap_high = [(i, i ^ (4 if i & 1 else 2)) for i in range(copies)]
    swap_low = [(i, i ^ (2 if i & 1 else 4)) for i in range(copies)]
    far_same = [[j + 8 * m for m in range(copies // 8)] for j in range(8)]

    def across(a, perm):
        return lax.ppermute(a, "replica", perm)

    def shifted(a, k):
        return lax.ppermute(a, "group", [(i, (i + k) % groups) for i in range(groups)])

    def on_device(tokens, segment, g_attn, w_qkv, w_out, g_mlp, w_in, w_down, grad_out):
        length = tokens.shape[0]
        z = lax.axis_index("group")
        r = lax.axis_index("replica")
        core, two, four = r & 1, (r >> 1) & 1, (r >> 2) & 1
        hb = jnp.where(core == 1, four, two)
        lb = jnp.where(core == 1, two, four)
        place = jnp.stack([z, hb, lb, core]).astype(jnp.int32)

        def joined(near, got, after=()):
            return run(join, "join", [shape((2,) + near.shape)], place, [near, got], (), after)[0]

        def spread(a, after=()):
            here = joined(a, across(a, swap_high), after)
            low = across(here, swap_low)
            return [here, low, across(here, swap_core), across(low, swap_core)]

        def grad_self(ins, plan, high, after=()):
            depth = ins[plan[0][0]].shape[1]
            widths = [ins[dy].shape[1] // 2 for _, _, dy, _ in plan]
            turned = pltpu.VMEM((depth, 2 * length), bf16)
            keep, send = run(
                functools.partial(grad_for_self, plan, groups), "grad_for_self",
                [shape((groups, high, sum(widths)))] * 2, place, ins,
                [turned, turned, pltpu.VMEM((2 * length, max(widths)), bf16)], after,
            )
            return keep, across(send, swap_high)

        def owners(keep, got, after=()):
            dims = keep.shape[1:]
            mine, *others = run(
                functools.partial(add_owners, groups), "add_owners",
                [shape(dims, f32)] + [shape(dims)] * (groups - 1), place, [keep, got],
                (), after,
            )
            return mine, [shifted(t, k + 1) for k, t in enumerate(others)]

        def summed(mine, got, after=()):
            kind = bf16 if copies == 8 else f32
            (total,) = run(
                functools.partial(sum_pieces, groups), "sum_pieces", [shape(mine.shape, kind)], place,
                [mine] + list(got), (), after,
            )
            if copies > 8:
                total = lax.psum(total, "replica", axis_index_groups=far_same).astype(bf16)
            return total

        count = 2 * g_attn.shape[0] // PAIR
        own_gains = jnp.pad(jnp.concatenate([g_attn, g_mlp]).reshape(count, PAIR), ((0, ROWS - count), (0, 0)))

        def cut(w, at, size):
            half = w.shape[1] // 2
            return lax.dynamic_slice(w, (at, half * core), (size, half))

        quarter = 2 * ROWS * hb + ROWS * lb
        qkv_piece = jnp.concatenate([cut(w_qkv, quarter, ROWS), own_gains], axis=1)
        down = cut(w_down, 144 * hb + 64 * lb, 80).reshape(5, 16, 3, PAIR).transpose(2, 1, 0, 3).reshape(ROWS, DOWN)
        mlp_piece = jnp.concatenate([cut(w_in, quarter, ROWS), cut(w_out, quarter, ROWS), down], axis=1)
        cosine, sine = rotary_tables(token_positions(segment))
        seg_col, seg_row = segment[:, None], segment[None, :]
        qkv_stack, far_gains = run(
            functools.partial(stack_pieces, groups - 1), "stack_pieces", [shape((groups - 1, ROWS, QKV)), shape((groups - 1, ROWS, PAIR))], place,
            [shifted(qkv_piece, k) for k in range(1, groups)], (), [cosine, sine],
        )
        mlp_far = [shifted(mlp_piece, k) for k in range(1, groups)]
        qkv_parts = spread(qkv_stack, mlp_far[:1])
        (mlp_stack,) = run(
            functools.partial(stack_pieces, groups - 1), "stack_pieces", [shape((groups - 1, ROWS, MLP))], place,
            list(mlp_far), (), qkv_parts[1:3],
        )
        by_distance = jnp.concatenate([own_gains[None], far_gains])[:, :count]
        by_distance = by_distance.reshape(groups, 2, g_attn.shape[0]).astype(f32)
        gains = jnp.concatenate(
            [
                lax.dynamic_index_in_dim(by_distance, lax.rem(z + groups - g, groups), keepdims=False)
                for g in range(groups)
            ],
            axis=1,
        )

        mlp_here = joined(mlp_stack, across(mlp_stack, swap_high), qkv_parts[3:])
        rope = [cosine, sine, seg_col, seg_row]
        attn_in, qkv, mixed, lse, attn_sent = run(
            functools.partial(attn_forward, groups), "attn_forward",
            [shape((length, D)), shape((length, 3 * D)), shape((length, D)), shape((length, PAIR), f32), shape((length, 2 * D))],
            place, [gains] + rope + [tokens, w_qkv] + qkv_parts,
            [pltpu.VMEM((D, 3 * D), bf16)], [mlp_here],
        )
        low = across(mlp_here, swap_low)
        (low,) = run(keep_copy, "keep_copy", [shape(low.shape)], place, [low], (), [mixed])
        mlp_parts = [mlp_here, low, across(mlp_here, swap_core), across(low, swap_core)]
        output, middle_grad, mixed_grad, branch_grad, hidden, mlp_in, gate_up_grad, for_other = run(
            functools.partial(feed_forward, groups), "feed_forward",
            [
                shape((length, D)), shape((length, D), f32), shape((length, D)), shape((length, D)),
                shape((length, FF)), shape((length, D)), shape((length, 2 * FF)), shape((length, SENT)),
            ],
            place, [gains, mixed, tokens, grad_out, w_in, w_out, w_down] + mlp_parts,
            [
                pltpu.VMEM((D, 2 * FF), bf16), pltpu.VMEM((D, D), bf16), pltpu.VMEM((FF, D), bf16),
                pltpu.VMEM((length, D), f32), pltpu.VMEM((length, FF), f32), pltpu.VMEM((length, FF), f32),
                pltpu.VMEM((length, D), f32),
            ],
        )
        from_other = across(for_other, swap_core)

        attn_other = across(attn_sent, swap_core)
        down_keep, down_got = grad_self(
            [hidden, grad_out, from_other], [(0, (2, HIDDEN), 1, (2, UPSTREAM))], 144
        )
        rest_keep, rest_got = grad_self(
            [mlp_in, gate_up_grad, mixed, branch_grad, from_other, attn_other],
            [(0, (4, MLP_IN), 1, (4, GATE_UP)), (2, (5, D), 3, (4, BRANCH))], 96, [down_keep],
        )
        qkv_grad, qkv_send = run(
            attn_backward, "attn_backward", [shape((length, 3 * D)), shape((length, QKV))],
            place, [qkv, lse, mixed_grad] + rope, (), [rest_keep],
        )
        qkv_other = across(qkv_send, swap_core)
        qkv_keep, qkv_got = grad_self(
            [attn_in, qkv_grad, attn_other, qkv_other], [(0, (2, 0), 1, (3, 0))], 96
        )
        mlp_keep, mlp_send = run(
            functools.partial(split_mlp, groups), "split_mlp", [shape((groups, ROWS, MLP))] * 2, place,
            [down_keep, down_got, rest_keep, rest_got],
            (), [qkv_keep],
        )
        mlp_got = across(mlp_send, swap_low)
        (tokens_grad,) = run(
            functools.partial(attn_in_backward, groups), "attn_in_backward", [shape((length, D))],
            place, [qkv_grad, middle_grad, gains] + [tokens, w_qkv] + qkv_parts,
            [pltpu.VMEM((D, 3 * D), bf16), pltpu.VMEM((length, D), f32)], [mlp_keep],
        )
        qkv_keep, qkv_send = run(
            functools.partial(split_qkv, groups), "split_qkv", [shape((groups, ROWS, QKV))] * 2, place,
            [qkv_keep, qkv_got], (), [tokens_grad],
        )
        qkv_got = across(qkv_send, swap_low)
        mlp_mine, mlp_others = owners(mlp_keep, mlp_got, [qkv_keep])
        qkv_mine, qkv_others = owners(qkv_keep, qkv_got, [mlp_mine])
        mlp_sum = summed(mlp_mine, mlp_others, [qkv_mine])
        qkv_sum = summed(qkv_mine, qkv_others, [mlp_sum])
        mlp_pair = joined(mlp_sum, across(mlp_sum, swap_low), [qkv_sum])
        qkv_pair = joined(qkv_sum, across(qkv_sum, swap_low), [mlp_pair])
        mlp_quarters = joined(mlp_pair, across(mlp_pair, swap_high), [qkv_pair])
        qkv_got = across(qkv_pair, swap_high)
        shard = w_in.shape[0]
        in_grad, out_grad, down_grad, gain_two_grad = run(
            place_mlp, "place_mlp",
            [shape((shard, 2 * FF), f32), shape((shard, D), f32), shape((w_down.shape[0], D), f32), shape((1, shard), f32)],
            place, [g_mlp.astype(f32)[None, :], mlp_quarters, across(mlp_quarters, swap_core), w_in],
            (), [qkv_pair],
        )
        qkv_quarters = joined(qkv_pair, qkv_got, [in_grad])
        qkv_weight_grad, gain_one_grad = run(
            place_qkv, "place_qkv", [shape((shard, 3 * D), f32), shape((1, shard), f32)], place,
            [g_attn.astype(f32)[None, :], qkv_quarters, across(qkv_quarters, swap_core), w_qkv],
            (), [in_grad],
        )
        return (
            output, tokens_grad, gain_one_grad[0], qkv_weight_grad, out_grad, gain_two_grad[0], in_grad, down_grad,
        )

    return on_device


def solution(mesh):
    both = ("replica", "group")
    in_specs = (
        P(both, None), P(both), P("group"), P("group", None), P("group", None),
        P("group"), P("group", None), P("group", None), P(both, None),
    )
    out_specs = (
        P(both, None), P(both, None), P("group"), P("group", None),
        P("group", None), P("group"), P("group", None), P("group", None),
    )
    return jax.shard_map(
        make(mesh), mesh=mesh, in_specs=in_specs, out_specs=out_specs, check_vma=False
    )
```

```python
import functools

import jax
import jax.numpy as jnp
from jax import lax
from jax.experimental import pallas as pl
from jax.experimental.pallas import tpu as pltpu
from jax.sharding import PartitionSpec as P

HEADS = 12
HEAD_DIM = 64
FF = 1152
D = 768
TILE = 384
PAIR = 128
ROWS = 48
QKV = 3 * D // 2
IN_OUT = FF + D // 2
DOWN = 640
MLP = IN_OUT + DOWN

norm_eps = 1e-05
rope_base = 160000.0
head_scale = HEAD_DIM ** (-0.5)
f32 = jnp.float32
bf16 = jnp.bfloat16

VMEM = pl.BlockSpec(memory_space=pltpu.VMEM)
SMEM = pl.BlockSpec(memory_space=pltpu.SMEM)
ANY = pl.BlockSpec(memory_space=pl.ANY)


def run(body, name, outs, place, ins, scratch=(), after=()):
    count, extra = len(ins), len(after)

    def inner(place, *refs):
        body(place, *refs[:count], *refs[count + extra :])

    return pl.pallas_call(
        inner,
        out_shape=outs,
        in_specs=[SMEM] + [VMEM] * count + [ANY] * extra,
        out_specs=[VMEM] * len(outs),
        scratch_shapes=list(scratch),
        compiler_params=pltpu.CompilerParams(vmem_limit_bytes=44 * 1024 * 1024),
        cost_estimate=pl.CostEstimate(flops=0, bytes_accessed=0, transcendentals=0),
        name=name,
    )(place, *ins, *after)


def shape(dims, dtype=bf16):
    return jax.ShapeDtypeStruct(dims, dtype)


def dot(a, b):
    return lax.dot_general(a, b, (((1,), (0,)), ((), ())), preferred_element_type=f32)


def dot_bt(a, b):
    return lax.dot_general(a, b, (((1,), (1,)), ((), ())), preferred_element_type=f32)


def dot_at(a, b):
    return lax.dot_general(a, b, (((0,), (0,)), ((), ())), preferred_element_type=f32)


def token_positions(segment):
    length = segment.shape[0]
    index = jnp.arange(length, dtype=jnp.int32)
    before = jnp.concatenate([jnp.full((1,), -1, jnp.int32), segment[:-1]])
    first = lax.cummax(jnp.where(segment != before, index, 0), axis=0)
    return index - first


def rotary_tables(position):
    half_dim = HEAD_DIM // 2
    inverse = rope_base ** (-(jnp.arange(half_dim, dtype=f32) * 2.0 / HEAD_DIM))
    angles = position.astype(f32)[:, None] * inverse[None, :]
    cosine, sine = jnp.cos(angles), jnp.sin(angles)
    return (
        jnp.concatenate([cosine] * 4, axis=1),
        jnp.concatenate([-sine, sine, -sine, sine], axis=1),
    )


def rows(start, size, step=16):
    return pl.ds(pl.multiple_of(start, step), size)


def columns(start, size):
    return pl.ds(pl.multiple_of(start, 128), size)


def piece_rows(place, flip_high, flip_low, other):
    hb, lb = place[1], place[2]
    return (lb if other else hb) ^ flip_high, (hb if other else lb) ^ flip_low


def each_part(groups, place, parts):
    for index, part in enumerate(parts):
        flip_low, other = index & 1, index >> 1
        for flip_high in range(2):
            hi, lo = piece_rows(place, flip_high, flip_low, other)
            for k in range(1, groups):
                owner = lax.rem(place[0] + groups - k, groups)
                yield part, flip_high, k - 1, owner, hi, lo, place[3] ^ other


def assemble(groups, place, parts, own, full, width, start):
    shard = own.shape[0]
    full[rows(place[0] * shard, shard), :] = own[...]
    for part, i, j, owner, hi, lo, half in each_part(groups, place, parts):
        at = owner * shard + hi * 2 * ROWS + lo * ROWS
        full[rows(at, ROWS), columns(half * width, width)] = part[i, j, :, start : start + width]


def packed_blocks():
    for i in range(5):
        for j in range(3):
            n = 3 * i + j
            yield i, 16 * i, PAIR * j, 16 * (n % 3), PAIR * (n // 3)


def norm_parts(values):
    centred = values - jnp.mean(values, axis=1, keepdims=True)
    inverse = lax.rsqrt(jnp.mean(centred * centred, axis=1, keepdims=True) + norm_eps)
    return centred * inverse, inverse


def norm_back(upstream, normed, inverse, gain):
    scaled = upstream * gain
    inner = (
        scaled
        - jnp.mean(scaled, axis=1, keepdims=True)
        - normed * jnp.mean(scaled * normed, axis=1, keepdims=True)
    )
    return inverse * inner


def swap_halves(u):
    lane = lax.broadcasted_iota(jnp.int32, u.shape, 1)
    return jnp.where(lane % HEAD_DIM < HEAD_DIM // 2, pltpu.roll(u, PAIR - 32, 1), pltpu.roll(u, 32, 1))


def copy_half(place, whole, half):
    width = whole.shape[1] // 2
    half[...] = whole[:, columns((1 - place[3]) * width, width)]


def head_masks():
    lane = lax.broadcasted_iota(jnp.int32, (1, PAIR), 1)
    first = (lane < HEAD_DIM).astype(f32)
    return first.astype(bf16), (1.0 - first).astype(bf16)


def attn_forward(groups, place, gains, cosine, sine, seg_col, seg_row, tok, own, *rest):
    parts, (attn_in, qkv, mixed, lse, for_other, w_full) = rest[:4], rest[4:]
    assemble(groups, place, parts, own, w_full, QKV, 0)
    normed, _ = norm_parts(tok[...].astype(f32))
    attn_in[...] = (normed * gains[0:1, :]).astype(bf16)

    def turned(j, _):
        at = columns(j * TILE, TILE)
        raw = dot(attn_in[...], w_full[:, at])
        turned_parts = []
        for i in range(TILE // PAIR):
            u = raw[:, i * PAIR : (i + 1) * PAIR]
            turned_parts.append(u * cosine[...] + swap_halves(u) * sine[...])
        qkv[:, at] = jnp.concatenate(turned_parts, axis=1).astype(bf16)
        return 0

    lax.fori_loop(0, 4, turned, 0)

    def plain(j, _):
        at = columns(j * TILE, TILE)
        qkv[:, at] = dot(attn_in[...], w_full[:, at]).astype(bf16)
        return 0

    lax.fori_loop(4, 6, plain, 0)
    masks = head_masks()
    same = seg_col[...] == seg_row[...]
    length = tok.shape[0]
    lane = lax.broadcasted_iota(jnp.int32, (length, PAIR), 1)

    def pair(j, kept):
        q = qkv[:, columns(j * PAIR, PAIR)]
        k = qkv[:, columns(D + j * PAIR, PAIR)]
        v = qkv[:, columns(2 * D + j * PAIR, PAIR)]
        made = []
        for a in range(2):
            scores = dot_bt(q * masks[a], k) * head_scale
            scores = jnp.where(same, scores, -1e30)
            top = jnp.max(scores, axis=1, keepdims=True)
            e = jnp.exp(scores - top)
            total = jnp.sum(e, axis=1, keepdims=True)
            probs = (e * (1.0 / total)).astype(bf16)
            made.append(dot(probs, v))
            kept = jnp.where(lane == 2 * j + a, top + jnp.log(total), kept)
        mixed[:, columns(j * PAIR, PAIR)] = jnp.where(lane < HEAD_DIM, made[0], made[1]).astype(bf16)
        return kept

    lse[...] = lax.fori_loop(0, HEADS // 2, pair, jnp.zeros((length, PAIR), f32), unroll=2)
    for_other[:, :D] = attn_in[...]
    for_other[:, D:] = mixed[...]


def feed_forward(groups, place, gains, mixed, tok, grad_out, own_in, own_out, own_down, *rest):
    parts, rest = rest[:4], rest[4:]
    output, middle_grad, mixed_grad, branch_grad, hidden, mlp_in, gate_up_grad, for_other, for_other_next = rest[:9]
    w_in, w_out, w_down, middle, act, slope, total = rest[9:]
    assemble(groups, place, parts, own_out, w_out, D // 2, FF)
    assemble(groups, place, parts, own_in, w_in, FF, 0)
    shard = own_down.shape[0]
    w_down[rows(place[0] * shard, shard), :] = own_down[...]
    for part, i, j, owner, hi, lo, half in each_part(groups, place, parts):
        base = owner * shard + hi * 144 + lo * 64
        for _, r, c, pr, pc in packed_blocks():
            block = part[i, j, pr : pr + 16, IN_OUT + pc : IN_OUT + pc + PAIR]
            w_down[rows(base + r, 16), columns(half * (D // 2) + c, PAIR)] = block

    for j in range(2):
        at = slice(j * TILE, (j + 1) * TILE)
        middle[:, at] = tok[:, at].astype(f32) + dot(mixed[...], w_out[:, at])
    normed, inverse = norm_parts(middle[...])
    mlp_in[...] = (normed * gains[1:2, :]).astype(bf16)

    def forward(j, _):
        at = columns(j * TILE, TILE)
        u = dot(mlp_in[...], w_in[:, at])
        gate = dot(mlp_in[...], w_in[:, columns(FF + j * TILE, TILE)])
        cdf = 0.5 + 0.5 * lax.erf(u * 0.7071067811865476)
        a = u * cdf
        act[:, at] = a
        slope[:, at] = gate * (cdf + u * (0.3989422804014327 * jnp.exp(-0.5 * u * u)))
        hidden[:, at] = (a * gate).astype(bf16)
        return 0

    lax.fori_loop(0, FF // TILE, forward, 0)

    def backward(j, _):
        at = columns(j * TILE, TILE)
        hidden_grad = dot_bt(grad_out[...], w_down[rows(j * TILE, TILE), :])
        gate_up_grad[:, at] = (hidden_grad * slope[:, at]).astype(bf16)
        gate_up_grad[:, columns(FF + j * TILE, TILE)] = (hidden_grad * act[:, at]).astype(bf16)
        return 0

    lax.fori_loop(0, FF // TILE, backward, 0)
    for j in range(2):
        at = slice(j * TILE, (j + 1) * TILE)
        output[:, at] = (middle[:, at] + dot(hidden[...], w_down[:, at])).astype(bf16)

    def step(j, _):
        total[:, columns(j * 256, 256)] = dot_bt(gate_up_grad[...], w_in[rows(j * 256, 256), :])
        return 0

    lax.fori_loop(0, D // 256, step, 0)
    normed, inverse = norm_parts(middle[...])
    part = norm_back(total[...], normed, inverse, gains[1:2, :])
    whole = grad_out[...].astype(f32) + part
    middle_grad[...] = whole
    branch_grad[...] = whole.astype(bf16)

    def back(j, _):
        mixed_grad[:, columns(j * 256, 256)] = dot_bt(
            branch_grad[...], w_out[rows(j * 256, 256), :]
        ).astype(bf16)
        return 0

    lax.fori_loop(0, D // 256, back, 0)
    for_other[:, :D] = mlp_in[...]
    copy_half(place, gate_up_grad, for_other.at[:, GATE_UP:BRANCH])
    copy_half(place, branch_grad, for_other.at[:, BRANCH:])
    for_other_next[:, :FF] = hidden[...]
    copy_half(place, grad_out, for_other_next.at[:, UPSTREAM:])


MLP_IN, GATE_UP, BRANCH, SENT_FIRST = 0, D, FF + D, FF + D + D // 2
HIDDEN, UPSTREAM, SENT_NEXT = 0, FF, FF + D // 2


def attn_backward(place, qkv, lse, mixed_grad, cosine, sine, seg_col, seg_row, qkv_grad, for_other):
    masks = head_masks()
    same = seg_col[...] == seg_row[...]
    length = qkv.shape[0]
    lane = lax.broadcasted_iota(jnp.int32, (length, PAIR), 1)

    def pair(j, _):
        q = qkv[:, columns(j * PAIR, PAIR)]
        k = qkv[:, columns(D + j * PAIR, PAIR)]
        v = qkv[:, columns(2 * D + j * PAIR, PAIR)]
        upstream = mixed_grad[:, columns(j * PAIR, PAIR)]
        made = []
        for a in range(2):
            scores = dot_bt(q * masks[a], k) * head_scale
            log_total = jnp.sum(jnp.where(lane == 2 * j + a, lse[...], 0.0), axis=1, keepdims=True)
            probs = jnp.where(same, jnp.exp(scores - log_total), 0.0)
            prob_grad = dot_bt(upstream * masks[a], v)
            delta = jnp.sum(probs * prob_grad, axis=1, keepdims=True)
            score_grad = (probs * (prob_grad - delta)).astype(bf16)
            made.append(
                (
                    dot(score_grad, k),
                    dot_at(score_grad, q),
                    dot_at(probs.astype(bf16), upstream),
                )
            )
        first = lane < HEAD_DIM
        for i in range(2):
            u = jnp.where(first, made[0][i], made[1][i]) * head_scale
            u = u * cosine[...] - swap_halves(u) * sine[...]
            qkv_grad[:, columns(i * D + j * PAIR, PAIR)] = u.astype(bf16)
        qkv_grad[:, columns(2 * D + j * PAIR, PAIR)] = jnp.where(first, made[0][2], made[1][2]).astype(bf16)
        return 0

    lax.fori_loop(0, HEADS // 2, pair, 0, unroll=2)
    copy_half(place, qkv_grad, for_other)


def attn_in_backward(groups, place, qkv_grad, middle_grad, gains, tok, own, *rest):
    parts, (tokens_grad, w_full, total) = rest[:4], rest[4:]
    assemble(groups, place, parts, own, w_full, QKV, 0)

    def step(j, _):
        total[:, columns(j * 256, 256)] = dot_bt(qkv_grad[...], w_full[rows(j * 256, 256), :])
        return 0

    lax.fori_loop(0, D // 256, step, 0)
    normed, inverse = norm_parts(tok[...].astype(f32))
    part = norm_back(total[...], normed, inverse, gains[0:1, :])
    tokens_grad[...] = (middle_grad[...] + part).astype(bf16)


def grad_for_self(plan, groups, place, *refs):
    ins, (keep, send, natural, ordered, right) = refs[:-5], refs[-5:]
    hb, core = place[1], place[3]
    high = keep.shape[1]
    cut = groups * high
    start = 0
    for x, (x_from, x_at), dy, (dy_from, dy_at) in plan:
        x, x_other, dy, dy_other = ins[x], ins[x_from], ins[dy], ins[dy_from]
        length, depth = x.shape
        half = dy.shape[1] // 2
        natural[:, :length] = x[...].T
        natural[:, length:] = x_other[:, x_at : x_at + depth].T
        for side in range(2):
            for g in range(groups):
                at = g * 2 * high + (hb ^ side) * high
                ordered[side * cut + g * high : side * cut + (g + 1) * high, :] = natural[rows(at, high), :]
        right[:length, :half] = dy[:, columns(core * half, half)]
        right[length:, :half] = dy_other[:, dy_at : dy_at + half]

        def step(t, _, start=start):
            made = dot(ordered[...], right[:, columns(t * TILE, TILE)])
            at = columns(start + t * TILE, TILE)
            for side, target in enumerate((keep, send)):
                for g in range(groups):
                    target[g, :, at] = made[side * cut + g * high : side * cut + (g + 1) * high, :].astype(bf16)
            return 0

        lax.fori_loop(0, half // TILE, step, 0)
        start += half


def split_mlp(groups, place, down, down_got, rest, rest_got, keep, send):
    lb = place[2]
    for side, target in enumerate((keep, send)):
        low, low_down = rows((lb ^ side) * ROWS, ROWS), rows((lb ^ side) * 64, 80)
        for g in range(groups):
            target[g, :, :IN_OUT] = (rest[g, low, :].astype(f32) + rest_got[g, low, :].astype(f32)).astype(bf16)
            made = (down[g, low_down, :].astype(f32) + down_got[g, low_down, :].astype(f32)).astype(bf16)
            for _, r, c, pr, pc in packed_blocks():
                target[g, pr : pr + 16, IN_OUT + pc : IN_OUT + pc + PAIR] = made[r : r + 16, c : c + PAIR]


def split_qkv(groups, place, mine, got, keep, send):
    for side, target in enumerate((keep, send)):
        low = rows((place[2] ^ side) * ROWS, ROWS)
        for g in range(groups):
            target[g] = (mine[g, low, :].astype(f32) + got[g, low, :].astype(f32)).astype(bf16)


def add_owners(groups, place, mine, got, *outs):
    for k in range(groups):
        g = lax.rem(place[0] + k, groups)
        outs[k][...] = (mine[g].astype(f32) + got[g].astype(f32)).astype(outs[k].dtype)


def sum_pieces(groups, place, mine, *refs):
    total = mine[...]
    for ref in refs[:-1]:
        total = total + ref[...].astype(f32)
    refs[-1][...] = total.astype(refs[-1].dtype)


def gain_grad(grad, weight, gain):
    ones = jnp.ones((8, grad.shape[1]), f32)
    summed = lax.dot_general(
        ones, grad * weight.astype(f32), (((1,), (1,)), ((), ())),
        precision=lax.Precision.HIGHEST, preferred_element_type=f32,
    )
    return summed[0:1, :] / gain


def place_mlp(place, gain, here, other, weight, in_grad, out_grad, down_grad, gain_out):
    for core, part in enumerate((here, other)):
        for flip_high in range(2):
            hi, lo = piece_rows(place, flip_high, 0, core)
            half = place[3] ^ core
            for flip_low in range(2):
                at = rows(hi * 2 * ROWS + (lo ^ flip_low) * ROWS, ROWS)
                piece = part[flip_high, flip_low]
                in_grad[at, columns(half * FF, FF)] = piece[:, :FF].astype(f32)
                out_grad[at, columns(half * (D // 2), D // 2)] = piece[:, FF:IN_OUT].astype(f32)
            one = part[flip_high, 0, :, IN_OUT:].astype(f32)
            two = part[flip_high, 1, :, IN_OUT:].astype(f32)
            low, up = jnp.where(lo == 0, one, two), jnp.where(lo == 0, two, one)
            for i, r, c, pr, pc in packed_blocks():
                at = columns(half * (D // 2) + c, PAIR)
                down_grad[rows(hi * 144 + r, 16), at] = low[pr : pr + 16, pc : pc + PAIR]
                if i > 0:
                    down_grad[rows(hi * 144 + 64 + r, 16), at] = up[pr : pr + 16, pc : pc + PAIR]
    gain_out[...] = gain_grad(in_grad[...], weight[...], gain[...])


def place_qkv(place, gain, here, other, weight, grad, gain_out):
    for core, part in enumerate((here, other)):
        for flip_high in range(2):
            for flip_low in range(2):
                hi, lo = piece_rows(place, flip_high, flip_low, core)
                at = rows(hi * 2 * ROWS + lo * ROWS, ROWS)
                grad[at, columns((place[3] ^ core) * QKV, QKV)] = part[flip_high, flip_low].astype(f32)
    gain_out[...] = gain_grad(grad[...], weight[...], gain[...])


def stack_pieces(count, place, *refs):
    for k, ref in enumerate(refs[:count]):
        start = 0
        for out in refs[count:]:
            width = out.shape[2]
            out[k] = ref[:, start : start + width]
            start += width


def keep_copy(place, given, out):
    out[...] = given[...]


def join(place, near, got, out):
    out[0] = near[...]
    out[1] = got[...]


def make(mesh):
    groups, copies = mesh.shape["group"], mesh.shape["replica"]
    swap_core = [(i, i ^ 1) for i in range(copies)]
    swap_high = [(i, i ^ (4 if i & 1 else 2)) for i in range(copies)]
    swap_low = [(i, i ^ (2 if i & 1 else 4)) for i in range(copies)]
    far_same = [[j + 8 * m for m in range(copies // 8)] for j in range(8)]

    def across(a, perm):
        return lax.ppermute(a, "replica", perm)

    def shifted(a, k):
        return lax.ppermute(a, "group", [(i, (i + k) % groups) for i in range(groups)])

    def on_device(tokens, segment, g_attn, w_qkv, w_out, g_mlp, w_in, w_down, grad_out):
        length = tokens.shape[0]
        z = lax.axis_index("group")
        r = lax.axis_index("replica")
        core, two, four = r & 1, (r >> 1) & 1, (r >> 2) & 1
        hb = jnp.where(core == 1, four, two)
        lb = jnp.where(core == 1, two, four)
        place = jnp.stack([z, hb, lb, core]).astype(jnp.int32)

        def joined(near, got, after=()):
            return run(join, "join", [shape((2,) + near.shape)], place, [near, got], (), after)[0]

        def spread(a, after=()):
            here = joined(a, across(a, swap_high), after)
            low = across(here, swap_low)
            return [here, low, across(here, swap_core), across(low, swap_core)]

        def grad_self(ins, plan, high, after=()):
            depth = ins[plan[0][0]].shape[1]
            widths = [ins[dy].shape[1] // 2 for _, _, dy, _ in plan]
            turned = pltpu.VMEM((depth, 2 * length), bf16)
            keep, send = run(
                functools.partial(grad_for_self, plan, groups), "grad_for_self",
                [shape((groups, high, sum(widths)))] * 2, place, ins,
                [turned, turned, pltpu.VMEM((2 * length, max(widths)), bf16)], after,
            )
            return keep, across(send, swap_high)

        def owners(keep, got, after=()):
            dims = keep.shape[1:]
            mine, *others = run(
                functools.partial(add_owners, groups), "add_owners",
                [shape(dims, f32)] + [shape(dims)] * (groups - 1), place, [keep, got],
                (), after,
            )
            return mine, [shifted(t, k + 1) for k, t in enumerate(others)]

        def summed(mine, got, after=()):
            kind = bf16 if copies == 8 else f32
            (total,) = run(
                functools.partial(sum_pieces, groups), "sum_pieces", [shape(mine.shape, kind)], place,
                [mine] + list(got), (), after,
            )
            if copies > 8:
                total = lax.psum(total, "replica", axis_index_groups=far_same).astype(bf16)
            return total

        count = 2 * g_attn.shape[0] // PAIR
        own_gains = jnp.pad(jnp.concatenate([g_attn, g_mlp]).reshape(count, PAIR), ((0, ROWS - count), (0, 0)))

        def cut(w, at, size):
            half = w.shape[1] // 2
            return lax.dynamic_slice(w, (at, half * core), (size, half))

        quarter = 2 * ROWS * hb + ROWS * lb
        qkv_piece = jnp.concatenate([cut(w_qkv, quarter, ROWS), own_gains], axis=1)
        down = cut(w_down, 144 * hb + 64 * lb, 80).reshape(5, 16, 3, PAIR).transpose(2, 1, 0, 3).reshape(ROWS, DOWN)
        mlp_piece = jnp.concatenate([cut(w_in, quarter, ROWS), cut(w_out, quarter, ROWS), down], axis=1)
        cosine, sine = rotary_tables(token_positions(segment))
        seg_col, seg_row = segment[:, None], segment[None, :]
        qkv_stack, far_gains = run(
            functools.partial(stack_pieces, groups - 1), "stack_pieces", [shape((groups - 1, ROWS, QKV)), shape((groups - 1, ROWS, PAIR))], place,
            [shifted(qkv_piece, k) for k in range(1, groups)], (), [cosine, sine],
        )
        mlp_far = [shifted(mlp_piece, k) for k in range(1, groups)]
        qkv_parts = spread(qkv_stack, mlp_far[:1])
        (mlp_stack,) = run(
            functools.partial(stack_pieces, groups - 1), "stack_pieces", [shape((groups - 1, ROWS, MLP))], place,
            list(mlp_far), (), qkv_parts[1:3],
        )
        by_distance = jnp.concatenate([own_gains[None], far_gains])[:, :count]
        by_distance = by_distance.reshape(groups, 2, g_attn.shape[0]).astype(f32)
        gains = jnp.concatenate(
            [
                lax.dynamic_index_in_dim(by_distance, lax.rem(z + groups - g, groups), keepdims=False)
                for g in range(groups)
            ],
            axis=1,
        )

        mlp_here = joined(mlp_stack, across(mlp_stack, swap_high), qkv_parts[3:])
        rope = [cosine, sine, seg_col, seg_row]
        attn_in, qkv, mixed, lse, attn_sent = run(
            functools.partial(attn_forward, groups), "attn_forward",
            [shape((length, D)), shape((length, 3 * D)), shape((length, D)), shape((length, PAIR), f32), shape((length, 2 * D))],
            place, [gains] + rope + [tokens, w_qkv] + qkv_parts,
            [pltpu.VMEM((D, 3 * D), bf16)], [mlp_here],
        )
        low = across(mlp_here, swap_low)
        (low,) = run(keep_copy, "keep_copy", [shape(low.shape)], place, [low], (), [mixed])
        mlp_parts = [mlp_here, low, across(mlp_here, swap_core), across(low, swap_core)]
        output, middle_grad, mixed_grad, branch_grad, hidden, mlp_in, gate_up_grad, for_other, for_other_next = run(
            functools.partial(feed_forward, groups), "feed_forward",
            [
                shape((length, D)), shape((length, D), f32), shape((length, D)), shape((length, D)),
                shape((length, FF)), shape((length, D)), shape((length, 2 * FF)), shape((length, SENT_FIRST)), shape((length, SENT_NEXT)),
            ],
            place, [gains, mixed, tokens, grad_out, w_in, w_out, w_down] + mlp_parts,
            [
                pltpu.VMEM((D, 2 * FF), bf16), pltpu.VMEM((D, D), bf16), pltpu.VMEM((FF, D), bf16),
                pltpu.VMEM((length, D), f32), pltpu.VMEM((length, FF), f32), pltpu.VMEM((length, FF), f32),
                pltpu.VMEM((length, D), f32),
            ],
        )
        from_other, from_other_next = across(for_other, swap_core), across(for_other_next, swap_core)

        attn_other = across(attn_sent, swap_core)
        rest_keep, rest_got = grad_self(
            [mlp_in, gate_up_grad, mixed, branch_grad, from_other, attn_other],
            [(0, (4, MLP_IN), 1, (4, GATE_UP)), (2, (5, D), 3, (4, BRANCH))], 96,
        )
        down_keep, down_got = grad_self(
            [hidden, grad_out, from_other_next], [(0, (2, HIDDEN), 1, (2, UPSTREAM))], 144, [rest_keep]
        )
        qkv_grad, qkv_send = run(
            attn_backward, "attn_backward", [shape((length, 3 * D)), shape((length, QKV))],
            place, [qkv, lse, mixed_grad] + rope, (), [down_keep],
        )
        qkv_other = across(qkv_send, swap_core)
        qkv_keep, qkv_got = grad_self(
            [attn_in, qkv_grad, attn_other, qkv_other], [(0, (2, 0), 1, (3, 0))], 96
        )
        mlp_keep, mlp_send = run(
            functools.partial(split_mlp, groups), "split_mlp", [shape((groups, ROWS, MLP))] * 2, place,
            [down_keep, down_got, rest_keep, rest_got],
            (), [qkv_keep],
        )
        mlp_got = across(mlp_send, swap_low)
        (tokens_grad,) = run(
            functools.partial(attn_in_backward, groups), "attn_in_backward", [shape((length, D))],
            place, [qkv_grad, middle_grad, gains] + [tokens, w_qkv] + qkv_parts,
            [pltpu.VMEM((D, 3 * D), bf16), pltpu.VMEM((length, D), f32)], [mlp_keep],
        )
        qkv_keep, qkv_send = run(
            functools.partial(split_qkv, groups), "split_qkv", [shape((groups, ROWS, QKV))] * 2, place,
            [qkv_keep, qkv_got], (), [tokens_grad],
        )
        qkv_got = across(qkv_send, swap_low)
        mlp_mine, mlp_others = owners(mlp_keep, mlp_got, [qkv_keep])
        qkv_mine, qkv_others = owners(qkv_keep, qkv_got, [mlp_mine])
        mlp_sum = summed(mlp_mine, mlp_others, [qkv_mine])
        qkv_sum = summed(qkv_mine, qkv_others, [mlp_sum])
        mlp_pair = joined(mlp_sum, across(mlp_sum, swap_low), [qkv_sum])
        qkv_pair = joined(qkv_sum, across(qkv_sum, swap_low), [mlp_pair])
        mlp_quarters = joined(mlp_pair, across(mlp_pair, swap_high), [qkv_pair])
        qkv_got = across(qkv_pair, swap_high)
        shard = w_in.shape[0]
        in_grad, out_grad, down_grad, gain_two_grad = run(
            place_mlp, "place_mlp",
            [shape((shard, 2 * FF), f32), shape((shard, D), f32), shape((w_down.shape[0], D), f32), shape((1, shard), f32)],
            place, [g_mlp.astype(f32)[None, :], mlp_quarters, across(mlp_quarters, swap_core), w_in],
            (), [qkv_pair],
        )
        qkv_quarters = joined(qkv_pair, qkv_got, [in_grad])
        qkv_weight_grad, gain_one_grad = run(
            place_qkv, "place_qkv", [shape((shard, 3 * D), f32), shape((1, shard), f32)], place,
            [g_attn.astype(f32)[None, :], qkv_quarters, across(qkv_quarters, swap_core), w_qkv],
            (), [in_grad],
        )
        return (
            output, tokens_grad, gain_one_grad[0], qkv_weight_grad, out_grad, gain_two_grad[0], in_grad, down_grad,
        )

    return on_device


def solution(mesh):
    both = ("replica", "group")
    in_specs = (
        P(both, None), P(both), P("group"), P("group", None), P("group", None),
        P("group"), P("group", None), P("group", None), P(both, None),
    )
    out_specs = (
        P(both, None), P(both, None), P("group"), P("group", None),
        P("group", None), P("group"), P("group", None), P("group", None),
    )
    return jax.shard_map(
        make(mesh), mesh=mesh, in_specs=in_specs, out_specs=out_specs, check_vma=False
    )
```

```python
import functools

import jax
import jax.numpy as jnp
from jax import lax
from jax.experimental import pallas as pl
from jax.experimental.pallas import tpu as pltpu
from jax.sharding import PartitionSpec as P

HEADS = 12
HEAD_DIM = 64
FF = 1152
D = 768
TILE = 384
PAIR = 128
ROWS = 48
QKV = 3 * D // 2
IN_OUT = FF + D // 2
DOWN = 640
MLP = IN_OUT + DOWN

norm_eps = 1e-05
rope_base = 160000.0
head_scale = HEAD_DIM ** (-0.5)
f32 = jnp.float32
bf16 = jnp.bfloat16

VMEM = pl.BlockSpec(memory_space=pltpu.VMEM)
SMEM = pl.BlockSpec(memory_space=pltpu.SMEM)
ANY = pl.BlockSpec(memory_space=pl.ANY)


def run(body, name, outs, place, ins, scratch=(), after=()):
    count, extra = len(ins), len(after)

    def inner(place, *refs):
        body(place, *refs[:count], *refs[count + extra :])

    return pl.pallas_call(
        inner,
        out_shape=outs,
        in_specs=[SMEM] + [VMEM] * count + [ANY] * extra,
        out_specs=[VMEM] * len(outs),
        scratch_shapes=list(scratch),
        compiler_params=pltpu.CompilerParams(vmem_limit_bytes=44 * 1024 * 1024),
        cost_estimate=pl.CostEstimate(flops=0, bytes_accessed=0, transcendentals=0),
        name=name,
    )(place, *ins, *after)


def shape(dims, dtype=bf16):
    return jax.ShapeDtypeStruct(dims, dtype)


def dot(a, b):
    return lax.dot_general(a, b, (((1,), (0,)), ((), ())), preferred_element_type=f32)


def dot_bt(a, b):
    return lax.dot_general(a, b, (((1,), (1,)), ((), ())), preferred_element_type=f32)


def dot_at(a, b):
    return lax.dot_general(a, b, (((0,), (0,)), ((), ())), preferred_element_type=f32)


def token_positions(segment):
    length = segment.shape[0]
    index = jnp.arange(length, dtype=jnp.int32)
    before = jnp.concatenate([jnp.full((1,), -1, jnp.int32), segment[:-1]])
    first = lax.cummax(jnp.where(segment != before, index, 0), axis=0)
    return index - first


def rotary_tables(position):
    half_dim = HEAD_DIM // 2
    inverse = rope_base ** (-(jnp.arange(half_dim, dtype=f32) * 2.0 / HEAD_DIM))
    angles = position.astype(f32)[:, None] * inverse[None, :]
    cosine, sine = jnp.cos(angles), jnp.sin(angles)
    return (
        jnp.concatenate([cosine] * 4, axis=1),
        jnp.concatenate([-sine, sine, -sine, sine], axis=1),
    )


def rows(start, size, step=16):
    return pl.ds(pl.multiple_of(start, step), size)


def columns(start, size):
    return pl.ds(pl.multiple_of(start, 128), size)


def piece_rows(place, flip_high, flip_low, other):
    hb, lb = place[1], place[2]
    return (lb if other else hb) ^ flip_high, (hb if other else lb) ^ flip_low


def each_part(groups, place, parts):
    for index, part in enumerate(parts):
        flip_low, other = index & 1, index >> 1
        for flip_high in range(2):
            hi, lo = piece_rows(place, flip_high, flip_low, other)
            for k in range(1, groups):
                owner = lax.rem(place[0] + groups - k, groups)
                yield part, flip_high, k - 1, owner, hi, lo, place[3] ^ other


def assemble(groups, place, parts, own, full, width, start):
    shard = own.shape[0]
    full[rows(place[0] * shard, shard), :] = own[...]
    for part, i, j, owner, hi, lo, half in each_part(groups, place, parts):
        at = owner * shard + hi * 2 * ROWS + lo * ROWS
        full[rows(at, ROWS), columns(half * width, width)] = part[i, j, :, start : start + width]


def packed_blocks():
    for i in range(5):
        for j in range(3):
            n = 3 * i + j
            yield i, 16 * i, PAIR * j, 16 * (n % 3), PAIR * (n // 3)


def norm_parts(values):
    centred = values - jnp.mean(values, axis=1, keepdims=True)
    inverse = lax.rsqrt(jnp.mean(centred * centred, axis=1, keepdims=True) + norm_eps)
    return centred * inverse, inverse


def norm_back(upstream, normed, inverse, gain):
    scaled = upstream * gain
    inner = (
        scaled
        - jnp.mean(scaled, axis=1, keepdims=True)
        - normed * jnp.mean(scaled * normed, axis=1, keepdims=True)
    )
    return inverse * inner


def swap_halves(u):
    lane = lax.broadcasted_iota(jnp.int32, u.shape, 1)
    return jnp.where(lane % HEAD_DIM < HEAD_DIM // 2, pltpu.roll(u, PAIR - 32, 1), pltpu.roll(u, 32, 1))


def copy_half(place, whole, half):
    width = whole.shape[1] // 2
    half[...] = whole[:, columns((1 - place[3]) * width, width)]


def head_masks():
    lane = lax.broadcasted_iota(jnp.int32, (1, PAIR), 1)
    first = (lane < HEAD_DIM).astype(f32)
    return first.astype(bf16), (1.0 - first).astype(bf16)


def attn_forward(groups, place, gains, cosine, sine, seg_col, seg_row, tok, own, *rest):
    parts, (attn_in, qkv, mixed, lse, for_other, w_full) = rest[:4], rest[4:]
    assemble(groups, place, parts, own, w_full, QKV, 0)
    normed, _ = norm_parts(tok[...].astype(f32))
    attn_in[...] = (normed * gains[0:1, :]).astype(bf16)

    def turned(j, _):
        at = columns(j * TILE, TILE)
        raw = dot(attn_in[...], w_full[:, at])
        turned_parts = []
        for i in range(TILE // PAIR):
            u = raw[:, i * PAIR : (i + 1) * PAIR]
            turned_parts.append(u * cosine[...] + swap_halves(u) * sine[...])
        qkv[:, at] = jnp.concatenate(turned_parts, axis=1).astype(bf16)
        return 0

    lax.fori_loop(0, 4, turned, 0)

    def plain(j, _):
        at = columns(j * TILE, TILE)
        qkv[:, at] = dot(attn_in[...], w_full[:, at]).astype(bf16)
        return 0

    lax.fori_loop(4, 6, plain, 0)
    masks = head_masks()
    same = seg_col[...] == seg_row[...]
    length = tok.shape[0]
    lane = lax.broadcasted_iota(jnp.int32, (length, PAIR), 1)

    def pair(j, kept):
        q = qkv[:, columns(j * PAIR, PAIR)]
        k = qkv[:, columns(D + j * PAIR, PAIR)]
        v = qkv[:, columns(2 * D + j * PAIR, PAIR)]
        made = []
        for a in range(2):
            scores = dot_bt(q * masks[a], k) * head_scale
            scores = jnp.where(same, scores, -1e30)
            top = jnp.max(scores, axis=1, keepdims=True)
            e = jnp.exp(scores - top)
            total = jnp.sum(e, axis=1, keepdims=True)
            probs = (e * (1.0 / total)).astype(bf16)
            made.append(dot(probs, v))
            kept = jnp.where(lane == 2 * j + a, top + jnp.log(total), kept)
        mixed[:, columns(j * PAIR, PAIR)] = jnp.where(lane < HEAD_DIM, made[0], made[1]).astype(bf16)
        return kept

    lse[...] = lax.fori_loop(0, HEADS // 2, pair, jnp.zeros((length, PAIR), f32), unroll=2)
    for_other[:, :D] = attn_in[...]
    for_other[:, D:] = mixed[...]


def feed_forward(groups, place, gains, mixed, tok, grad_out, own_in, own_out, own_down, *rest):
    parts, rest = rest[:4], rest[4:]
    output, middle_grad, mixed_grad, branch_grad, hidden, mlp_in, gate_up_grad, for_other, for_other_next = rest[:9]
    w_in, w_out, w_down, middle, act, slope, total = rest[9:]
    assemble(groups, place, parts, own_out, w_out, D // 2, FF)
    assemble(groups, place, parts, own_in, w_in, FF, 0)
    shard = own_down.shape[0]
    w_down[rows(place[0] * shard, shard), :] = own_down[...]
    for part, i, j, owner, hi, lo, half in each_part(groups, place, parts):
        base = owner * shard + hi * 144 + lo * 64
        for _, r, c, pr, pc in packed_blocks():
            block = part[i, j, pr : pr + 16, IN_OUT + pc : IN_OUT + pc + PAIR]
            w_down[rows(base + r, 16), columns(half * (D // 2) + c, PAIR)] = block

    for j in range(2):
        at = slice(j * TILE, (j + 1) * TILE)
        middle[:, at] = tok[:, at].astype(f32) + dot(mixed[...], w_out[:, at])
    normed, inverse = norm_parts(middle[...])
    mlp_in[...] = (normed * gains[1:2, :]).astype(bf16)

    def forward(j, _):
        at = columns(j * TILE, TILE)
        u = dot(mlp_in[...], w_in[:, at])
        gate = dot(mlp_in[...], w_in[:, columns(FF + j * TILE, TILE)])
        cdf = 0.5 + 0.5 * lax.erf(u * 0.7071067811865476)
        a = u * cdf
        act[:, at] = a
        slope[:, at] = gate * (cdf + u * (0.3989422804014327 * jnp.exp(-0.5 * u * u)))
        hidden[:, at] = (a * gate).astype(bf16)
        return 0

    lax.fori_loop(0, FF // TILE, forward, 0, unroll=True)

    def backward(j, _):
        at = columns(j * TILE, TILE)
        hidden_grad = dot_bt(grad_out[...], w_down[rows(j * TILE, TILE), :])
        gate_up_grad[:, at] = (hidden_grad * slope[:, at]).astype(bf16)
        gate_up_grad[:, columns(FF + j * TILE, TILE)] = (hidden_grad * act[:, at]).astype(bf16)
        return 0

    lax.fori_loop(0, FF // TILE, backward, 0, unroll=True)
    for j in range(2):
        at = slice(j * TILE, (j + 1) * TILE)
        output[:, at] = (middle[:, at] + dot(hidden[...], w_down[:, at])).astype(bf16)

    def step(j, _):
        total[:, columns(j * 256, 256)] = dot_bt(gate_up_grad[...], w_in[rows(j * 256, 256), :])
        return 0

    lax.fori_loop(0, D // 256, step, 0, unroll=True)
    normed, inverse = norm_parts(middle[...])
    part = norm_back(total[...], normed, inverse, gains[1:2, :])
    whole = grad_out[...].astype(f32) + part
    middle_grad[...] = whole
    branch_grad[...] = whole.astype(bf16)

    def back(j, _):
        mixed_grad[:, columns(j * 256, 256)] = dot_bt(
            branch_grad[...], w_out[rows(j * 256, 256), :]
        ).astype(bf16)
        return 0

    lax.fori_loop(0, D // 256, back, 0, unroll=True)
    for_other[:, :D] = mlp_in[...]
    copy_half(place, gate_up_grad, for_other.at[:, GATE_UP:BRANCH])
    copy_half(place, branch_grad, for_other.at[:, BRANCH:])
    for_other_next[:, :FF] = hidden[...]
    copy_half(place, grad_out, for_other_next.at[:, UPSTREAM:])


MLP_IN, GATE_UP, BRANCH, SENT_FIRST = 0, D, FF + D, FF + D + D // 2
HIDDEN, UPSTREAM, SENT_NEXT = 0, FF, FF + D // 2


def attn_backward(place, qkv, lse, mixed_grad, cosine, sine, seg_col, seg_row, qkv_grad, for_other):
    masks = head_masks()
    same = seg_col[...] == seg_row[...]
    length = qkv.shape[0]
    lane = lax.broadcasted_iota(jnp.int32, (length, PAIR), 1)

    def pair(j, _):
        q = qkv[:, columns(j * PAIR, PAIR)]
        k = qkv[:, columns(D + j * PAIR, PAIR)]
        v = qkv[:, columns(2 * D + j * PAIR, PAIR)]
        upstream = mixed_grad[:, columns(j * PAIR, PAIR)]
        made = []
        for a in range(2):
            scores = dot_bt(q * masks[a], k) * head_scale
            log_total = jnp.sum(jnp.where(lane == 2 * j + a, lse[...], 0.0), axis=1, keepdims=True)
            probs = jnp.where(same, jnp.exp(scores - log_total), 0.0)
            prob_grad = dot_bt(upstream * masks[a], v)
            delta = jnp.sum(probs * prob_grad, axis=1, keepdims=True)
            score_grad = (probs * (prob_grad - delta)).astype(bf16)
            made.append(
                (
                    dot(score_grad, k),
                    dot_at(score_grad, q),
                    dot_at(probs.astype(bf16), upstream),
                )
            )
        first = lane < HEAD_DIM
        for i in range(2):
            u = jnp.where(first, made[0][i], made[1][i]) * head_scale
            u = u * cosine[...] - swap_halves(u) * sine[...]
            qkv_grad[:, columns(i * D + j * PAIR, PAIR)] = u.astype(bf16)
        qkv_grad[:, columns(2 * D + j * PAIR, PAIR)] = jnp.where(first, made[0][2], made[1][2]).astype(bf16)
        return 0

    lax.fori_loop(0, HEADS // 2, pair, 0, unroll=2)
    copy_half(place, qkv_grad, for_other)


def attn_in_backward(groups, place, qkv_grad, middle_grad, gains, tok, own, *rest):
    parts, (tokens_grad, w_full, total) = rest[:4], rest[4:]
    assemble(groups, place, parts, own, w_full, QKV, 0)

    def step(j, _):
        total[:, columns(j * 256, 256)] = dot_bt(qkv_grad[...], w_full[rows(j * 256, 256), :])
        return 0

    lax.fori_loop(0, D // 256, step, 0, unroll=True)
    normed, inverse = norm_parts(tok[...].astype(f32))
    part = norm_back(total[...], normed, inverse, gains[0:1, :])
    tokens_grad[...] = (middle_grad[...] + part).astype(bf16)


def grad_for_self(plan, groups, place, *refs):
    ins, (keep, send, natural, ordered, right) = refs[:-5], refs[-5:]
    hb, core = place[1], place[3]
    high = keep.shape[1]
    cut = groups * high
    start = 0
    for x, (x_from, x_at), dy, (dy_from, dy_at) in plan:
        x, x_other, dy, dy_other = ins[x], ins[x_from], ins[dy], ins[dy_from]
        length, depth = x.shape
        half = dy.shape[1] // 2
        natural[:, :length] = x[...].T
        natural[:, length:] = x_other[:, x_at : x_at + depth].T
        for side in range(2):
            for g in range(groups):
                at = g * 2 * high + (hb ^ side) * high
                ordered[side * cut + g * high : side * cut + (g + 1) * high, :] = natural[rows(at, high), :]
        right[:length, :half] = dy[:, columns(core * half, half)]
        right[length:, :half] = dy_other[:, dy_at : dy_at + half]

        def step(t, _, start=start):
            made = dot(ordered[...], right[:, columns(t * TILE, TILE)])
            at = columns(start + t * TILE, TILE)
            for side, target in enumerate((keep, send)):
                for g in range(groups):
                    target[g, :, at] = made[side * cut + g * high : side * cut + (g + 1) * high, :].astype(bf16)
            return 0

        lax.fori_loop(0, half // TILE, step, 0, unroll=True)
        start += half


def split_mlp(groups, place, down, down_got, rest, rest_got, keep, send):
    lb = place[2]
    for side, target in enumerate((keep, send)):
        low, low_down = rows((lb ^ side) * ROWS, ROWS), rows((lb ^ side) * 64, 80)
        for g in range(groups):
            target[g, :, :IN_OUT] = (rest[g, low, :].astype(f32) + rest_got[g, low, :].astype(f32)).astype(bf16)
            made = (down[g, low_down, :].astype(f32) + down_got[g, low_down, :].astype(f32)).astype(bf16)
            for _, r, c, pr, pc in packed_blocks():
                target[g, pr : pr + 16, IN_OUT + pc : IN_OUT + pc + PAIR] = made[r : r + 16, c : c + PAIR]


def split_qkv(groups, place, mine, got, keep, send):
    for side, target in enumerate((keep, send)):
        low = rows((place[2] ^ side) * ROWS, ROWS)
        for g in range(groups):
            target[g] = (mine[g, low, :].astype(f32) + got[g, low, :].astype(f32)).astype(bf16)


def add_owners(groups, place, mine, got, *outs):
    for k in range(groups):
        g = lax.rem(place[0] + k, groups)
        outs[k][...] = (mine[g].astype(f32) + got[g].astype(f32)).astype(outs[k].dtype)


def sum_pieces(groups, place, mine, *refs):
    total = mine[...]
    for ref in refs[:-1]:
        total = total + ref[...].astype(f32)
    refs[-1][...] = total.astype(refs[-1].dtype)


def gain_grad(grad, weight, gain):
    summed = jnp.sum(grad * weight.astype(f32), axis=1, keepdims=True)
    return jnp.broadcast_to(summed, (grad.shape[0], PAIR)).T[0:1, :] / gain


def place_mlp(place, gain, here, other, weight, in_grad, out_grad, down_grad, gain_out):
    for core, part in enumerate((here, other)):
        for flip_high in range(2):
            hi, lo = piece_rows(place, flip_high, 0, core)
            half = place[3] ^ core
            for flip_low in range(2):
                at = rows(hi * 2 * ROWS + (lo ^ flip_low) * ROWS, ROWS)
                piece = part[flip_high, flip_low]
                in_grad[at, columns(half * FF, FF)] = piece[:, :FF].astype(f32)
                out_grad[at, columns(half * (D // 2), D // 2)] = piece[:, FF:IN_OUT].astype(f32)
            one = part[flip_high, 0, :, IN_OUT:].astype(f32)
            two = part[flip_high, 1, :, IN_OUT:].astype(f32)
            low, up = jnp.where(lo == 0, one, two), jnp.where(lo == 0, two, one)
            for i, r, c, pr, pc in packed_blocks():
                at = columns(half * (D // 2) + c, PAIR)
                down_grad[rows(hi * 144 + r, 16), at] = low[pr : pr + 16, pc : pc + PAIR]
                if i > 0:
                    down_grad[rows(hi * 144 + 64 + r, 16), at] = up[pr : pr + 16, pc : pc + PAIR]
    gain_out[...] = gain_grad(in_grad[...], weight[...], gain[...])


def place_qkv(place, gain, here, other, weight, grad, gain_out):
    for core, part in enumerate((here, other)):
        for flip_high in range(2):
            for flip_low in range(2):
                hi, lo = piece_rows(place, flip_high, flip_low, core)
                at = rows(hi * 2 * ROWS + lo * ROWS, ROWS)
                grad[at, columns((place[3] ^ core) * QKV, QKV)] = part[flip_high, flip_low].astype(f32)
    gain_out[...] = gain_grad(grad[...], weight[...], gain[...])


def stack_pieces(count, place, *refs):
    for k, ref in enumerate(refs[:count]):
        start = 0
        for out in refs[count:]:
            width = out.shape[2]
            out[k] = ref[:, start : start + width]
            start += width


def keep_copy(place, given, out):
    out[...] = given[...]


def join(place, near, got, out):
    out[0] = near[...]
    out[1] = got[...]


def make(mesh):
    groups, copies = mesh.shape["group"], mesh.shape["replica"]
    swap_core = [(i, i ^ 1) for i in range(copies)]
    swap_high = [(i, i ^ (4 if i & 1 else 2)) for i in range(copies)]
    swap_low = [(i, i ^ (2 if i & 1 else 4)) for i in range(copies)]
    far_same = [[j + 8 * m for m in range(copies // 8)] for j in range(8)]

    def across(a, perm):
        return lax.ppermute(a, "replica", perm)

    def shifted(a, k):
        return lax.ppermute(a, "group", [(i, (i + k) % groups) for i in range(groups)])

    def on_device(tokens, segment, g_attn, w_qkv, w_out, g_mlp, w_in, w_down, grad_out):
        length = tokens.shape[0]
        z = lax.axis_index("group")
        r = lax.axis_index("replica")
        core, two, four = r & 1, (r >> 1) & 1, (r >> 2) & 1
        hb = jnp.where(core == 1, four, two)
        lb = jnp.where(core == 1, two, four)
        place = jnp.stack([z, hb, lb, core]).astype(jnp.int32)

        def joined(near, got, after=()):
            return run(join, "join", [shape((2,) + near.shape)], place, [near, got], (), after)[0]

        def spread(a, after=()):
            here = joined(a, across(a, swap_high), after)
            low = across(here, swap_low)
            return [here, low, across(here, swap_core), across(low, swap_core)]

        def grad_self(ins, plan, high, after=()):
            depth = ins[plan[0][0]].shape[1]
            widths = [ins[dy].shape[1] // 2 for _, _, dy, _ in plan]
            turned = pltpu.VMEM((depth, 2 * length), bf16)
            keep, send = run(
                functools.partial(grad_for_self, plan, groups), "grad_for_self",
                [shape((groups, high, sum(widths)))] * 2, place, ins,
                [turned, turned, pltpu.VMEM((2 * length, max(widths)), bf16)], after,
            )
            return keep, across(send, swap_high)

        def owners(keep, got, after=()):
            dims = keep.shape[1:]
            mine, *others = run(
                functools.partial(add_owners, groups), "add_owners",
                [shape(dims, f32)] + [shape(dims)] * (groups - 1), place, [keep, got],
                (), after,
            )
            return mine, [shifted(t, k + 1) for k, t in enumerate(others)]

        def summed(mine, got, after=()):
            kind = bf16 if copies == 8 else f32
            (total,) = run(
                functools.partial(sum_pieces, groups), "sum_pieces", [shape(mine.shape, kind)], place,
                [mine] + list(got), (), after,
            )
            if copies > 8:
                total = lax.psum(total, "replica", axis_index_groups=far_same).astype(bf16)
            return total

        count = 2 * g_attn.shape[0] // PAIR
        own_gains = jnp.pad(jnp.concatenate([g_attn, g_mlp]).reshape(count, PAIR), ((0, ROWS - count), (0, 0)))

        def cut(w, at, size):
            half = w.shape[1] // 2
            return lax.dynamic_slice(w, (at, half * core), (size, half))

        quarter = 2 * ROWS * hb + ROWS * lb
        qkv_piece = jnp.concatenate([cut(w_qkv, quarter, ROWS), own_gains], axis=1)
        down = cut(w_down, 144 * hb + 64 * lb, 80).reshape(5, 16, 3, PAIR).transpose(2, 1, 0, 3).reshape(ROWS, DOWN)
        mlp_piece = jnp.concatenate([cut(w_in, quarter, ROWS), cut(w_out, quarter, ROWS), down], axis=1)
        cosine, sine = rotary_tables(token_positions(segment))
        seg_col, seg_row = segment[:, None], segment[None, :]
        qkv_stack, far_gains = run(
            functools.partial(stack_pieces, groups - 1), "stack_pieces", [shape((groups - 1, ROWS, QKV)), shape((groups - 1, ROWS, PAIR))], place,
            [shifted(qkv_piece, k) for k in range(1, groups)], (), [cosine, sine],
        )
        mlp_far = [shifted(mlp_piece, k) for k in range(1, groups)]
        qkv_parts = spread(qkv_stack, mlp_far[:1])
        (mlp_stack,) = run(
            functools.partial(stack_pieces, groups - 1), "stack_pieces", [shape((groups - 1, ROWS, MLP))], place,
            list(mlp_far), (), qkv_parts[1:3],
        )
        by_distance = jnp.concatenate([own_gains[None], far_gains])[:, :count]
        by_distance = by_distance.reshape(groups, 2, g_attn.shape[0]).astype(f32)
        gains = jnp.concatenate(
            [
                lax.dynamic_index_in_dim(by_distance, lax.rem(z + groups - g, groups), keepdims=False)
                for g in range(groups)
            ],
            axis=1,
        )

        mlp_here = joined(mlp_stack, across(mlp_stack, swap_high), qkv_parts[3:])
        rope = [cosine, sine, seg_col, seg_row]
        attn_in, qkv, mixed, lse, attn_sent = run(
            functools.partial(attn_forward, groups), "attn_forward",
            [shape((length, D)), shape((length, 3 * D)), shape((length, D)), shape((length, PAIR), f32), shape((length, 2 * D))],
            place, [gains] + rope + [tokens, w_qkv] + qkv_parts,
            [pltpu.VMEM((D, 3 * D), bf16)], [mlp_here],
        )
        low = across(mlp_here, swap_low)
        (low,) = run(keep_copy, "keep_copy", [shape(low.shape)], place, [low], (), [mixed])
        mlp_parts = [mlp_here, low, across(mlp_here, swap_core), across(low, swap_core)]
        output, middle_grad, mixed_grad, branch_grad, hidden, mlp_in, gate_up_grad, for_other, for_other_next = run(
            functools.partial(feed_forward, groups), "feed_forward",
            [
                shape((length, D)), shape((length, D), f32), shape((length, D)), shape((length, D)),
                shape((length, FF)), shape((length, D)), shape((length, 2 * FF)), shape((length, SENT_FIRST)), shape((length, SENT_NEXT)),
            ],
            place, [gains, mixed, tokens, grad_out, w_in, w_out, w_down] + mlp_parts,
            [
                pltpu.VMEM((D, 2 * FF), bf16), pltpu.VMEM((D, D), bf16), pltpu.VMEM((FF, D), bf16),
                pltpu.VMEM((length, D), f32), pltpu.VMEM((length, FF), f32), pltpu.VMEM((length, FF), f32),
                pltpu.VMEM((length, D), f32),
            ],
        )
        from_other, from_other_next = across(for_other, swap_core), across(for_other_next, swap_core)

        attn_other = across(attn_sent, swap_core)
        rest_keep, rest_got = grad_self(
            [mlp_in, gate_up_grad, mixed, branch_grad, from_other, attn_other],
            [(0, (4, MLP_IN), 1, (4, GATE_UP)), (2, (5, D), 3, (4, BRANCH))], 96,
        )
        down_keep, down_got = grad_self(
            [hidden, grad_out, from_other_next], [(0, (2, HIDDEN), 1, (2, UPSTREAM))], 144, [rest_keep]
        )
        qkv_grad, qkv_send = run(
            attn_backward, "attn_backward", [shape((length, 3 * D)), shape((length, QKV))],
            place, [qkv, lse, mixed_grad] + rope, (), [down_keep],
        )
        qkv_other = across(qkv_send, swap_core)
        qkv_keep, qkv_got = grad_self(
            [attn_in, qkv_grad, attn_other, qkv_other], [(0, (2, 0), 1, (3, 0))], 96
        )
        mlp_keep, mlp_send = run(
            functools.partial(split_mlp, groups), "split_mlp", [shape((groups, ROWS, MLP))] * 2, place,
            [down_keep, down_got, rest_keep, rest_got],
            (), [qkv_keep],
        )
        mlp_got = across(mlp_send, swap_low)
        (tokens_grad,) = run(
            functools.partial(attn_in_backward, groups), "attn_in_backward", [shape((length, D))],
            place, [qkv_grad, middle_grad, gains] + [tokens, w_qkv] + qkv_parts,
            [pltpu.VMEM((D, 3 * D), bf16), pltpu.VMEM((length, D), f32)], [mlp_keep],
        )
        qkv_keep, qkv_send = run(
            functools.partial(split_qkv, groups), "split_qkv", [shape((groups, ROWS, QKV))] * 2, place,
            [qkv_keep, qkv_got], (), [tokens_grad],
        )
        qkv_got = across(qkv_send, swap_low)
        mlp_mine, mlp_others = owners(mlp_keep, mlp_got, [qkv_keep])
        qkv_mine, qkv_others = owners(qkv_keep, qkv_got, [mlp_mine])
        mlp_sum = summed(mlp_mine, mlp_others, [qkv_mine])
        qkv_sum = summed(qkv_mine, qkv_others, [mlp_sum])
        mlp_pair = joined(mlp_sum, across(mlp_sum, swap_low), [qkv_sum])
        qkv_pair = joined(qkv_sum, across(qkv_sum, swap_low), [mlp_pair])
        mlp_quarters = joined(mlp_pair, across(mlp_pair, swap_high), [qkv_pair])
        qkv_got = across(qkv_pair, swap_high)
        shard = w_in.shape[0]
        in_grad, out_grad, down_grad, gain_two_grad = run(
            place_mlp, "place_mlp",
            [shape((shard, 2 * FF), f32), shape((shard, D), f32), shape((w_down.shape[0], D), f32), shape((1, shard), f32)],
            place, [g_mlp.astype(f32)[None, :], mlp_quarters, across(mlp_quarters, swap_core), w_in],
            (), [qkv_pair],
        )
        qkv_quarters = joined(qkv_pair, qkv_got, [in_grad])
        qkv_weight_grad, gain_one_grad = run(
            place_qkv, "place_qkv", [shape((shard, 3 * D), f32), shape((1, shard), f32)], place,
            [g_attn.astype(f32)[None, :], qkv_quarters, across(qkv_quarters, swap_core), w_qkv],
            (), [in_grad],
        )
        return (
            output, tokens_grad, gain_one_grad[0], qkv_weight_grad, out_grad, gain_two_grad[0], in_grad, down_grad,
        )

    return on_device


def solution(mesh):
    both = ("replica", "group")
    in_specs = (
        P(both, None), P(both), P("group"), P("group", None), P("group", None),
        P("group"), P("group", None), P("group", None), P(both, None),
    )
    out_specs = (
        P(both, None), P(both, None), P("group"), P("group", None),
        P("group", None), P("group"), P("group", None), P("group", None),
    )
    return jax.shard_map(
        make(mesh), mesh=mesh, in_specs=in_specs, out_specs=out_specs, check_vma=False
    )
```

```python
import functools

import jax
import jax.numpy as jnp
from jax import lax
from jax.experimental import pallas as pl
from jax.experimental.pallas import tpu as pltpu
from jax.sharding import PartitionSpec as P

HEADS = 12
HEAD_DIM = 64
FF = 1152
D = 768
TILE = 384
PAIR = 128
ROWS = 48
QKV = 3 * D // 2
IN_OUT = FF + D // 2
DOWN = 640
MLP = IN_OUT + DOWN

norm_eps = 1e-05
rope_base = 160000.0
head_scale = HEAD_DIM ** (-0.5)
f32 = jnp.float32
bf16 = jnp.bfloat16

VMEM = pl.BlockSpec(memory_space=pltpu.VMEM)
SMEM = pl.BlockSpec(memory_space=pltpu.SMEM)
ANY = pl.BlockSpec(memory_space=pl.ANY)


def run(body, name, outs, place, ins, scratch=(), after=()):
    count, extra = len(ins), len(after)

    def inner(place, *refs):
        body(place, *refs[:count], *refs[count + extra :])

    return pl.pallas_call(
        inner,
        out_shape=outs,
        in_specs=[SMEM] + [VMEM] * count + [ANY] * extra,
        out_specs=[VMEM] * len(outs),
        scratch_shapes=list(scratch),
        compiler_params=pltpu.CompilerParams(vmem_limit_bytes=44 * 1024 * 1024),
        cost_estimate=pl.CostEstimate(flops=0, bytes_accessed=0, transcendentals=0),
        name=name,
    )(place, *ins, *after)


def shape(dims, dtype=bf16):
    return jax.ShapeDtypeStruct(dims, dtype)


def dot(a, b):
    return lax.dot_general(a, b, (((1,), (0,)), ((), ())), preferred_element_type=f32)


def dot_bt(a, b):
    return lax.dot_general(a, b, (((1,), (1,)), ((), ())), preferred_element_type=f32)


def dot_at(a, b):
    return lax.dot_general(a, b, (((0,), (0,)), ((), ())), preferred_element_type=f32)


def token_positions(segment):
    length = segment.shape[0]
    index = jnp.arange(length, dtype=jnp.int32)
    before = jnp.concatenate([jnp.full((1,), -1, jnp.int32), segment[:-1]])
    first = lax.cummax(jnp.where(segment != before, index, 0), axis=0)
    return index - first


def rotary_tables(position):
    half_dim = HEAD_DIM // 2
    inverse = rope_base ** (-(jnp.arange(half_dim, dtype=f32) * 2.0 / HEAD_DIM))
    angles = position.astype(f32)[:, None] * inverse[None, :]
    cosine, sine = jnp.cos(angles), jnp.sin(angles)
    return (
        jnp.concatenate([cosine] * 4, axis=1),
        jnp.concatenate([-sine, sine, -sine, sine], axis=1),
    )


def rows(start, size, step=16):
    return pl.ds(pl.multiple_of(start, step), size)


def columns(start, size):
    return pl.ds(pl.multiple_of(start, 128), size)


def piece_rows(place, flip_high, flip_low, other):
    hb, lb = place[1], place[2]
    return (lb if other else hb) ^ flip_high, (hb if other else lb) ^ flip_low


def each_part(groups, place, parts):
    for index, part in enumerate(parts):
        flip_low, other = index & 1, index >> 1
        for flip_high in range(2):
            hi, lo = piece_rows(place, flip_high, flip_low, other)
            for k in range(1, groups):
                owner = lax.rem(place[0] + groups - k, groups)
                yield part, flip_high, k - 1, owner, hi, lo, place[3] ^ other


def assemble(groups, place, parts, own, full, width, start):
    shard = own.shape[0]
    full[rows(place[0] * shard, shard), :] = own[...]
    for part, i, j, owner, hi, lo, half in each_part(groups, place, parts):
        at = owner * shard + hi * 2 * ROWS + lo * ROWS
        full[rows(at, ROWS), columns(half * width, width)] = part[i, j, :, start : start + width]


def packed_blocks():
    for i in range(5):
        for j in range(3):
            n = 3 * i + j
            yield i, 16 * i, PAIR * j, 16 * (n % 3), PAIR * (n // 3)


def norm_parts(values):
    centred = values - jnp.mean(values, axis=1, keepdims=True)
    inverse = lax.rsqrt(jnp.mean(centred * centred, axis=1, keepdims=True) + norm_eps)
    return centred * inverse, inverse


def norm_back(upstream, normed, inverse, gain):
    scaled = upstream * gain
    inner = (
        scaled
        - jnp.mean(scaled, axis=1, keepdims=True)
        - normed * jnp.mean(scaled * normed, axis=1, keepdims=True)
    )
    return inverse * inner


def swap_halves(u):
    lane = lax.broadcasted_iota(jnp.int32, u.shape, 1)
    return jnp.where(lane % HEAD_DIM < HEAD_DIM // 2, pltpu.roll(u, PAIR - 32, 1), pltpu.roll(u, 32, 1))


def copy_half(place, whole, half):
    width = whole.shape[1] // 2
    half[...] = whole[:, columns((1 - place[3]) * width, width)]


def head_masks():
    lane = lax.broadcasted_iota(jnp.int32, (1, PAIR), 1)
    first = (lane < HEAD_DIM).astype(f32)
    return first.astype(bf16), (1.0 - first).astype(bf16)


def attn_forward(groups, place, gains, cosine, sine, seg_col, seg_row, tok, own, *rest):
    parts, (attn_in, qkv, mixed, lse, for_other, w_full) = rest[:4], rest[4:]
    assemble(groups, place, parts, own, w_full, QKV, 0)
    normed, _ = norm_parts(tok[...].astype(f32))
    attn_in[...] = (normed * gains[0:1, :]).astype(bf16)

    def turned(j, _):
        at = columns(j * TILE, TILE)
        raw = dot(attn_in[...], w_full[:, at])
        turned_parts = []
        for i in range(TILE // PAIR):
            u = raw[:, i * PAIR : (i + 1) * PAIR]
            turned_parts.append(u * cosine[...] + swap_halves(u) * sine[...])
        qkv[:, at] = jnp.concatenate(turned_parts, axis=1).astype(bf16)
        return 0

    lax.fori_loop(0, 4, turned, 0)

    def plain(j, _):
        at = columns(j * TILE, TILE)
        qkv[:, at] = dot(attn_in[...], w_full[:, at]).astype(bf16)
        return 0

    lax.fori_loop(4, 6, plain, 0)
    masks = head_masks()
    same = seg_col[...] == seg_row[...]
    length = tok.shape[0]
    lane = lax.broadcasted_iota(jnp.int32, (length, PAIR), 1)

    def pair(j, kept):
        q = qkv[:, columns(j * PAIR, PAIR)]
        k = qkv[:, columns(D + j * PAIR, PAIR)]
        v = qkv[:, columns(2 * D + j * PAIR, PAIR)]
        made = []
        for a in range(2):
            scores = dot_bt(q * masks[a], k) * head_scale
            scores = jnp.where(same, scores, -1e30)
            top = jnp.max(scores, axis=1, keepdims=True)
            e = jnp.exp(scores - top)
            total = jnp.sum(e, axis=1, keepdims=True)
            probs = (e * (1.0 / total)).astype(bf16)
            made.append(dot(probs, v))
            kept = jnp.where(lane == 2 * j + a, top + jnp.log(total), kept)
        mixed[:, columns(j * PAIR, PAIR)] = jnp.where(lane < HEAD_DIM, made[0], made[1]).astype(bf16)
        return kept

    lse[...] = lax.fori_loop(0, HEADS // 2, pair, jnp.zeros((length, PAIR), f32), unroll=2)
    for_other[:, :D] = attn_in[...]
    for_other[:, D:] = mixed[...]


def feed_forward(groups, place, gains, mixed, tok, grad_out, own_in, own_out, own_down, *rest):
    parts, rest = rest[:4], rest[4:]
    output, middle_grad, mixed_grad, branch_grad, hidden, mlp_in, gate_up_grad, for_other, for_other_next = rest[:9]
    w_in, w_out, w_down, middle, act, slope, total = rest[9:]
    assemble(groups, place, parts, own_out, w_out, D // 2, FF)
    assemble(groups, place, parts, own_in, w_in, FF, 0)
    shard = own_down.shape[0]
    w_down[rows(place[0] * shard, shard), :] = own_down[...]
    for part, i, j, owner, hi, lo, half in each_part(groups, place, parts):
        base = owner * shard + hi * 144 + lo * 64
        for _, r, c, pr, pc in packed_blocks():
            block = part[i, j, pr : pr + 16, IN_OUT + pc : IN_OUT + pc + PAIR]
            w_down[rows(base + r, 16), columns(half * (D // 2) + c, PAIR)] = block

    for j in range(2):
        at = slice(j * TILE, (j + 1) * TILE)
        middle[:, at] = tok[:, at].astype(f32) + dot(mixed[...], w_out[:, at])
    normed, inverse = norm_parts(middle[...])
    mlp_in[...] = (normed * gains[1:2, :]).astype(bf16)

    def forward(j, _):
        at = columns(j * TILE, TILE)
        u = dot(mlp_in[...], w_in[:, at])
        gate = dot(mlp_in[...], w_in[:, columns(FF + j * TILE, TILE)])
        cdf = 0.5 + 0.5 * lax.erf(u * 0.7071067811865476)
        a = u * cdf
        act[:, at] = a
        slope[:, at] = gate * (cdf + u * (0.3989422804014327 * jnp.exp(-0.5 * u * u)))
        hidden[:, at] = (a * gate).astype(bf16)
        return 0

    lax.fori_loop(0, FF // TILE, forward, 0, unroll=True)

    def backward(j, _):
        at = columns(j * TILE, TILE)
        hidden_grad = dot_bt(grad_out[...], w_down[rows(j * TILE, TILE), :])
        gate_up_grad[:, at] = (hidden_grad * slope[:, at]).astype(bf16)
        gate_up_grad[:, columns(FF + j * TILE, TILE)] = (hidden_grad * act[:, at]).astype(bf16)
        return 0

    lax.fori_loop(0, FF // TILE, backward, 0, unroll=True)
    for j in range(2):
        at = slice(j * TILE, (j + 1) * TILE)
        output[:, at] = (middle[:, at] + dot(hidden[...], w_down[:, at])).astype(bf16)

    def step(j, _):
        total[:, columns(j * 256, 256)] = dot_bt(gate_up_grad[...], w_in[rows(j * 256, 256), :])
        return 0

    lax.fori_loop(0, D // 256, step, 0, unroll=True)
    normed, inverse = norm_parts(middle[...])
    part = norm_back(total[...], normed, inverse, gains[1:2, :])
    whole = grad_out[...].astype(f32) + part
    middle_grad[...] = whole
    branch_grad[...] = whole.astype(bf16)

    def back(j, _):
        mixed_grad[:, columns(j * 256, 256)] = dot_bt(
            branch_grad[...], w_out[rows(j * 256, 256), :]
        ).astype(bf16)
        return 0

    lax.fori_loop(0, D // 256, back, 0, unroll=True)
    for_other[:, :D] = mlp_in[...]
    copy_half(place, gate_up_grad, for_other.at[:, GATE_UP:BRANCH])
    copy_half(place, branch_grad, for_other.at[:, BRANCH:])
    for_other_next[:, :FF] = hidden[...]
    copy_half(place, grad_out, for_other_next.at[:, UPSTREAM:])


MLP_IN, GATE_UP, BRANCH, SENT_FIRST = 0, D, FF + D, FF + D + D // 2
HIDDEN, UPSTREAM, SENT_NEXT = 0, FF, FF + D // 2


def attn_backward(place, qkv, lse, mixed_grad, cosine, sine, seg_col, seg_row, qkv_grad, for_other):
    masks = head_masks()
    same = seg_col[...] == seg_row[...]
    length = qkv.shape[0]
    lane = lax.broadcasted_iota(jnp.int32, (length, PAIR), 1)

    def pair(j, _):
        q = qkv[:, columns(j * PAIR, PAIR)]
        k = qkv[:, columns(D + j * PAIR, PAIR)]
        v = qkv[:, columns(2 * D + j * PAIR, PAIR)]
        upstream = mixed_grad[:, columns(j * PAIR, PAIR)]
        made = []
        for a in range(2):
            scores = dot_bt(q * masks[a], k) * head_scale
            log_total = jnp.sum(jnp.where(lane == 2 * j + a, lse[...], 0.0), axis=1, keepdims=True)
            probs = jnp.where(same, jnp.exp(scores - log_total), 0.0)
            prob_grad = dot_bt(upstream * masks[a], v)
            delta = jnp.sum(probs * prob_grad, axis=1, keepdims=True)
            score_grad = (probs * (prob_grad - delta)).astype(bf16)
            made.append(
                (
                    dot(score_grad, k),
                    dot_at(score_grad, q),
                    dot_at(probs.astype(bf16), upstream),
                )
            )
        first = lane < HEAD_DIM
        for i in range(2):
            u = jnp.where(first, made[0][i], made[1][i]) * head_scale
            u = u * cosine[...] - swap_halves(u) * sine[...]
            qkv_grad[:, columns(i * D + j * PAIR, PAIR)] = u.astype(bf16)
        qkv_grad[:, columns(2 * D + j * PAIR, PAIR)] = jnp.where(first, made[0][2], made[1][2]).astype(bf16)
        return 0

    lax.fori_loop(0, HEADS // 2, pair, 0, unroll=2)
    copy_half(place, qkv_grad, for_other)


def attn_in_backward(groups, place, qkv_grad, middle_grad, gains, tok, own, *rest):
    parts, (tokens_grad, w_full, total) = rest[:4], rest[4:]
    assemble(groups, place, parts, own, w_full, QKV, 0)

    def step(j, _):
        total[:, columns(j * 256, 256)] = dot_bt(qkv_grad[...], w_full[rows(j * 256, 256), :])
        return 0

    lax.fori_loop(0, D // 256, step, 0, unroll=True)
    normed, inverse = norm_parts(tok[...].astype(f32))
    part = norm_back(total[...], normed, inverse, gains[0:1, :])
    tokens_grad[...] = (middle_grad[...] + part).astype(bf16)


def grad_for_self(plan, groups, place, *refs):
    ins, (keep, send, natural, ordered, right) = refs[:-5], refs[-5:]
    hb, core = place[1], place[3]
    high = keep.shape[1]
    cut = groups * high
    start = 0
    for x, (x_from, x_at), dy, (dy_from, dy_at) in plan:
        x, x_other, dy, dy_other = ins[x], ins[x_from], ins[dy], ins[dy_from]
        length, depth = x.shape
        half = dy.shape[1] // 2
        natural[:, :length] = x[...].T
        natural[:, length:] = x_other[:, x_at : x_at + depth].T
        for side in range(2):
            for g in range(groups):
                at = g * 2 * high + (hb ^ side) * high
                ordered[side * cut + g * high : side * cut + (g + 1) * high, :] = natural[rows(at, high), :]
        right[:length, :half] = dy[:, columns(core * half, half)]
        right[length:, :half] = dy_other[:, dy_at : dy_at + half]

        def step(t, _, start=start):
            made = dot(ordered[...], right[:, columns(t * TILE, TILE)])
            at = columns(start + t * TILE, TILE)
            for side, target in enumerate((keep, send)):
                for g in range(groups):
                    target[g, :, at] = made[side * cut + g * high : side * cut + (g + 1) * high, :].astype(bf16)
            return 0

        lax.fori_loop(0, half // TILE, step, 0, unroll=True)
        start += half


def split_mlp(groups, place, down, down_got, rest, rest_got, keep, send):
    lb = place[2]
    for side, target in enumerate((keep, send)):
        low, low_down = rows((lb ^ side) * ROWS, ROWS), rows((lb ^ side) * 64, 80)
        for g in range(groups):
            target[g, :, :IN_OUT] = (rest[g, low, :].astype(f32) + rest_got[g, low, :].astype(f32)).astype(bf16)
            made = (down[g, low_down, :].astype(f32) + down_got[g, low_down, :].astype(f32)).astype(bf16)
            for _, r, c, pr, pc in packed_blocks():
                target[g, pr : pr + 16, IN_OUT + pc : IN_OUT + pc + PAIR] = made[r : r + 16, c : c + PAIR]


def split_qkv(groups, place, mine, got, keep, send):
    for side, target in enumerate((keep, send)):
        low = rows((place[2] ^ side) * ROWS, ROWS)
        for g in range(groups):
            target[g] = (mine[g, low, :].astype(f32) + got[g, low, :].astype(f32)).astype(bf16)


def add_owners(groups, place, mine, got, *outs):
    for k in range(groups):
        g = lax.rem(place[0] + k, groups)
        outs[k][...] = (mine[g].astype(f32) + got[g].astype(f32)).astype(outs[k].dtype)


def sum_pieces(groups, place, mine, *refs):
    total = mine[...]
    for ref in refs[:-1]:
        total = total + ref[...].astype(f32)
    refs[-1][...] = total.astype(refs[-1].dtype)


def gain_grad(grad, weight, gain):
    summed = jnp.sum(grad * weight.astype(f32), axis=1, keepdims=True)
    return jnp.broadcast_to(summed, (grad.shape[0], PAIR)).T[0:1, :] / gain


def place_mlp(place, gain, here, other, weight, _, in_grad, out_grad, down_grad, gain_out):
    for core, part in enumerate((here, other)):
        for flip_high in range(2):
            hi, lo = piece_rows(place, flip_high, 0, core)
            half = place[3] ^ core
            for flip_low in range(2):
                at = rows(hi * 2 * ROWS + (lo ^ flip_low) * ROWS, ROWS)
                piece = part[flip_high, flip_low]
                in_grad[at, columns(half * FF, FF)] = piece[:, :FF].astype(f32)
                out_grad[at, columns(half * (D // 2), D // 2)] = piece[:, FF:IN_OUT].astype(f32)
            one = part[flip_high, 0, :, IN_OUT:].astype(f32)
            two = part[flip_high, 1, :, IN_OUT:].astype(f32)
            low, up = jnp.where(lo == 0, one, two), jnp.where(lo == 0, two, one)
            for i, r, c, pr, pc in packed_blocks():
                at = columns(half * (D // 2) + c, PAIR)
                down_grad[rows(hi * 144 + r, 16), at] = low[pr : pr + 16, pc : pc + PAIR]
                if i > 0:
                    down_grad[rows(hi * 144 + 64 + r, 16), at] = up[pr : pr + 16, pc : pc + PAIR]
    gain_out[...] = gain_grad(in_grad[...], weight[...], gain[...])


def place_qkv(place, gain, here, other, weight, grad, gain_out):
    for core, part in enumerate((here, other)):
        for flip_high in range(2):
            for flip_low in range(2):
                hi, lo = piece_rows(place, flip_high, flip_low, core)
                at = rows(hi * 2 * ROWS + lo * ROWS, ROWS)
                grad[at, columns((place[3] ^ core) * QKV, QKV)] = part[flip_high, flip_low].astype(f32)
    gain_out[...] = gain_grad(grad[...], weight[...], gain[...])


def stack_pieces(count, place, *refs):
    for k, ref in enumerate(refs[:count]):
        start = 0
        for out in refs[count:]:
            width = out.shape[2]
            out[k] = ref[:, start : start + width]
            start += width


def keep_copy(place, given, out):
    out[...] = given[...]


def join(place, near, got, out):
    out[0] = near[...]
    out[1] = got[...]


def make(mesh):
    groups, copies = mesh.shape["group"], mesh.shape["replica"]
    swap_core = [(i, i ^ 1) for i in range(copies)]
    swap_high = [(i, i ^ (4 if i & 1 else 2)) for i in range(copies)]
    swap_low = [(i, i ^ (2 if i & 1 else 4)) for i in range(copies)]
    far_same = [[j + 8 * m for m in range(copies // 8)] for j in range(8)]

    def across(a, perm):
        return lax.ppermute(a, "replica", perm)

    def shifted(a, k):
        return lax.ppermute(a, "group", [(i, (i + k) % groups) for i in range(groups)])

    def on_device(tokens, segment, g_attn, w_qkv, w_out, g_mlp, w_in, w_down, grad_out):
        length = tokens.shape[0]
        z = lax.axis_index("group")
        r = lax.axis_index("replica")
        core, two, four = r & 1, (r >> 1) & 1, (r >> 2) & 1
        hb = jnp.where(core == 1, four, two)
        lb = jnp.where(core == 1, two, four)
        place = jnp.stack([z, hb, lb, core]).astype(jnp.int32)

        def joined(near, got, after=()):
            return run(join, "join", [shape((2,) + near.shape)], place, [near, got], (), after)[0]

        def spread(a, after=()):
            here = joined(a, across(a, swap_high), after)
            low = across(here, swap_low)
            return [here, low, across(here, swap_core), across(low, swap_core)]

        def grad_self(ins, plan, high, after=()):
            depth = ins[plan[0][0]].shape[1]
            widths = [ins[dy].shape[1] // 2 for _, _, dy, _ in plan]
            turned = pltpu.VMEM((depth, 2 * length), bf16)
            keep, send = run(
                functools.partial(grad_for_self, plan, groups), "grad_for_self",
                [shape((groups, high, sum(widths)))] * 2, place, ins,
                [turned, turned, pltpu.VMEM((2 * length, max(widths)), bf16)], after,
            )
            return keep, across(send, swap_high)

        def owners(keep, got, after=()):
            dims = keep.shape[1:]
            mine, *others = run(
                functools.partial(add_owners, groups), "add_owners",
                [shape(dims, f32)] + [shape(dims)] * (groups - 1), place, [keep, got],
                (), after,
            )
            return mine, [shifted(t, k + 1) for k, t in enumerate(others)]

        def summed(mine, got, after=()):
            kind = bf16 if copies == 8 else f32
            (total,) = run(
                functools.partial(sum_pieces, groups), "sum_pieces", [shape(mine.shape, kind)], place,
                [mine] + list(got), (), after,
            )
            if copies > 8:
                total = lax.psum(total, "replica", axis_index_groups=far_same).astype(bf16)
            return total

        count = 2 * g_attn.shape[0] // PAIR
        own_gains = jnp.pad(jnp.concatenate([g_attn, g_mlp]).reshape(count, PAIR), ((0, ROWS - count), (0, 0)))

        def cut(w, at, size):
            half = w.shape[1] // 2
            return lax.dynamic_slice(w, (at, half * core), (size, half))

        quarter = 2 * ROWS * hb + ROWS * lb
        qkv_piece = jnp.concatenate([cut(w_qkv, quarter, ROWS), own_gains], axis=1)
        down = cut(w_down, 144 * hb + 64 * lb, 80).reshape(5, 16, 3, PAIR).transpose(2, 1, 0, 3).reshape(ROWS, DOWN)
        mlp_piece = jnp.concatenate([cut(w_in, quarter, ROWS), cut(w_out, quarter, ROWS), down], axis=1)
        cosine, sine = rotary_tables(token_positions(segment))
        seg_col, seg_row = segment[:, None], segment[None, :]
        qkv_stack, far_gains = run(
            functools.partial(stack_pieces, groups - 1), "stack_pieces", [shape((groups - 1, ROWS, QKV)), shape((groups - 1, ROWS, PAIR))], place,
            [shifted(qkv_piece, k) for k in range(1, groups)], (), [cosine, sine],
        )
        mlp_far = [shifted(mlp_piece, k) for k in range(1, groups)]
        qkv_parts = spread(qkv_stack, mlp_far[:1])
        (mlp_stack,) = run(
            functools.partial(stack_pieces, groups - 1), "stack_pieces", [shape((groups - 1, ROWS, MLP))], place,
            list(mlp_far), (), qkv_parts[1:3],
        )
        by_distance = jnp.concatenate([own_gains[None], far_gains])[:, :count]
        by_distance = by_distance.reshape(groups, 2, g_attn.shape[0]).astype(f32)
        gains = jnp.concatenate(
            [
                lax.dynamic_index_in_dim(by_distance, lax.rem(z + groups - g, groups), keepdims=False)
                for g in range(groups)
            ],
            axis=1,
        )

        mlp_here = joined(mlp_stack, across(mlp_stack, swap_high), qkv_parts[3:])
        rope = [cosine, sine, seg_col, seg_row]
        attn_in, qkv, mixed, lse, attn_sent = run(
            functools.partial(attn_forward, groups), "attn_forward",
            [shape((length, D)), shape((length, 3 * D)), shape((length, D)), shape((length, PAIR), f32), shape((length, 2 * D))],
            place, [gains] + rope + [tokens, w_qkv] + qkv_parts,
            [pltpu.VMEM((D, 3 * D), bf16)], [mlp_here],
        )
        low = across(mlp_here, swap_low)
        (low,) = run(keep_copy, "keep_copy", [shape(low.shape)], place, [low], (), [mixed])
        mlp_parts = [mlp_here, low, across(mlp_here, swap_core), across(low, swap_core)]
        output, middle_grad, mixed_grad, branch_grad, hidden, mlp_in, gate_up_grad, for_other, for_other_next = run(
            functools.partial(feed_forward, groups), "feed_forward",
            [
                shape((length, D)), shape((length, D), f32), shape((length, D)), shape((length, D)),
                shape((length, FF)), shape((length, D)), shape((length, 2 * FF)), shape((length, SENT_FIRST)), shape((length, SENT_NEXT)),
            ],
            place, [gains, mixed, tokens, grad_out, w_in, w_out, w_down] + mlp_parts,
            [
                pltpu.VMEM((D, 2 * FF), bf16), pltpu.VMEM((D, D), bf16), pltpu.VMEM((FF, D), bf16),
                pltpu.VMEM((length, D), f32), pltpu.VMEM((length, FF), f32), pltpu.VMEM((length, FF), f32),
                pltpu.VMEM((length, D), f32),
            ],
        )
        from_other, from_other_next = across(for_other, swap_core), across(for_other_next, swap_core)

        attn_other = across(attn_sent, swap_core)
        rest_keep, rest_got = grad_self(
            [mlp_in, gate_up_grad, mixed, branch_grad, from_other, attn_other],
            [(0, (4, MLP_IN), 1, (4, GATE_UP)), (2, (5, D), 3, (4, BRANCH))], 96,
        )
        down_keep, down_got = grad_self(
            [hidden, grad_out, from_other_next], [(0, (2, HIDDEN), 1, (2, UPSTREAM))], 144, [rest_keep]
        )
        qkv_grad, qkv_send = run(
            attn_backward, "attn_backward", [shape((length, 3 * D)), shape((length, QKV))],
            place, [qkv, lse, mixed_grad] + rope, (), [down_keep],
        )
        qkv_other = across(qkv_send, swap_core)
        qkv_keep, qkv_got = grad_self(
            [attn_in, qkv_grad, attn_other, qkv_other], [(0, (2, 0), 1, (3, 0))], 96
        )
        mlp_keep, mlp_send = run(
            functools.partial(split_mlp, groups), "split_mlp", [shape((groups, ROWS, MLP))] * 2, place,
            [down_keep, down_got, rest_keep, rest_got],
            (), [qkv_keep],
        )
        mlp_got = across(mlp_send, swap_low)
        (tokens_grad,) = run(
            functools.partial(attn_in_backward, groups), "attn_in_backward", [shape((length, D))],
            place, [qkv_grad, middle_grad, gains] + [tokens, w_qkv] + qkv_parts,
            [pltpu.VMEM((D, 3 * D), bf16), pltpu.VMEM((length, D), f32)], [mlp_keep],
        )
        qkv_keep, qkv_send = run(
            functools.partial(split_qkv, groups), "split_qkv", [shape((groups, ROWS, QKV))] * 2, place,
            [qkv_keep, qkv_got], (), [tokens_grad],
        )
        qkv_got = across(qkv_send, swap_low)
        mlp_mine, mlp_others = owners(mlp_keep, mlp_got, [qkv_keep])
        qkv_mine, qkv_others = owners(qkv_keep, qkv_got, [mlp_mine])
        mlp_sum = summed(mlp_mine, mlp_others, [qkv_mine])
        qkv_sum = summed(qkv_mine, qkv_others, [mlp_sum])
        mlp_pair = joined(mlp_sum, across(mlp_sum, swap_low), [qkv_sum])
        qkv_pair = joined(qkv_sum, across(qkv_sum, swap_low), [mlp_pair])
        mlp_quarters = joined(mlp_pair, across(mlp_pair, swap_high), [qkv_pair])
        qkv_got = across(qkv_pair, swap_high)
        shard = w_in.shape[0]
        in_grad, out_grad, down_grad, gain_two_grad = run(
            place_mlp, "place_mlp",
            [shape((shard, 2 * FF), f32), shape((shard, D), f32), shape((w_down.shape[0], D), f32), shape((1, shard), f32)],
            place, [g_mlp.astype(f32)[None, :], mlp_quarters, across(mlp_quarters, swap_core), w_in, w_qkv],
            (), [qkv_pair],
        )
        qkv_quarters = joined(qkv_pair, qkv_got, [in_grad])
        qkv_weight_grad, gain_one_grad = run(
            place_qkv, "place_qkv", [shape((shard, 3 * D), f32), shape((1, shard), f32)], place,
            [g_attn.astype(f32)[None, :], qkv_quarters, across(qkv_quarters, swap_core), w_qkv],
            (), [in_grad],
        )
        return (
            output, tokens_grad, gain_one_grad[0], qkv_weight_grad, out_grad, gain_two_grad[0], in_grad, down_grad,
        )

    return on_device


def solution(mesh):
    both = ("replica", "group")
    in_specs = (
        P(both, None), P(both), P("group"), P("group", None), P("group", None),
        P("group"), P("group", None), P("group", None), P(both, None),
    )
    out_specs = (
        P(both, None), P(both, None), P("group"), P("group", None),
        P("group", None), P("group"), P("group", None), P("group", None),
    )
    return jax.shard_map(
        make(mesh), mesh=mesh, in_specs=in_specs, out_specs=out_specs, check_vma=False
    )
```
